32 devices in a mesh: row: 4 (over y, core), col: 2 (over x), blk: 4 (over z).
Axes of the slice: x: 2, y: 2, z: 4, core: 2. Of those that a mesh axis runs over, the one named last changes fastest.
Arguments:
- pixels: bfloat16 [256, 64, 1024], P('row', 'col', 'blk'), may hold values from -6 to 6
- dw_kernel: float32 [7, 7, 1024], P(None, None, 'blk'), may hold values from -4 to 4
- dw_bias: float32 [1024], P('blk'), may hold values from -3 to 3
- ln_gain: float32 [1024], P('blk'), may hold values from 0.25 to 1.75
- ln_bias: float32 [1024], P('blk'), may hold values from -2 to 2
- w_in: bfloat16 [4096, 1024], P('blk'), may hold values from -0.1875 to 0.1875
- b_in: bfloat16 [4096], P('blk'), may hold values from -2 to 2
- w_out: bfloat16 [4096, 1024], P('blk'), may hold values from -0.125 to 0.125
- b_out: float32 [1024], P('blk'), may hold values from -2 to 2
- layer_scale: float32 [1024], P('blk'), may hold values from 0.5 to 2
Outputs:
- block_out: bfloat16 [256, 64, 1024], P('row', 'col', 'blk')
The draws below stay inside these ranges and needn't reach their ends.
All inputs are finite; a program needn't handle non-finite values.
Results may differ from the reference program's by a relative error of at most 0.012.
Values may be sent and summed in bfloat16 or wider, within the bound.
A program may use at most 64 MiB of HBM per device.

```python
import math
import jax
import jax.numpy as jnp
from jax import lax

C = 1024
HID = 4096
KS = 7
H = 256
W = 64
N_BLK = 4


def draw_dw_kernel(key, part):
    key_vals = jax.random.fold_in(key, 11)
    key_scale = jax.random.fold_in(key, 12)
    key_order = jax.random.fold_in(key, 13)
    order = jax.random.permutation(key_order, C).astype(jnp.float32)
    rising = 3.0 ** (order / (C - 1))
    factor = jnp.exp(jax.random.uniform(key_scale, (C,), jnp.float32, 0.0, 1.19))
    values = jax.random.normal(key_vals, (KS, KS, C), jnp.float32)
    return jnp.clip(values * rising * factor / 7.0, -4.0, 4.0)


def draw_pixels(key, part):
    key_vals = jax.random.fold_in(key, 21)
    key_gain = jax.random.fold_in(key, 22)
    key_shift = jax.random.fold_in(key, 23)
    group_gain = jnp.exp(jax.random.uniform(key_gain, (16,), jnp.float32, -1.2, 1.2))
    group_shift = jax.random.uniform(key_shift, (16,), jnp.float32, -0.8, 0.8)
    gains = jnp.repeat(group_gain, C // 16)
    shifts = jnp.repeat(group_shift, C // 16)
    values = jax.random.normal(key_vals, (H, W, C), jnp.float32) * gains + shifts
    return jnp.clip(values, -6.0, 6.0).astype(jnp.bfloat16)


def raised(entries, own_key, source, target, blocks, factor):
    owner, partner = [(jnp.arange(entries.shape[axis_at]) // (entries.shape[axis_at] // blocks)).reshape([-1 if axis == axis_at else 1 for axis in range(entries.ndim)]) for axis_at in (source, target)]
    chosen = jax.random.permutation(own_key, blocks)[partner]
    strong = (owner == chosen) | (owner == (partner + blocks // 2) % blocks)
    return jnp.where(strong, factor * entries, entries)


def block_scale(key, dims, cuts, least, top_value):
    gain, own = 1.0, jax.random.fold_in(key, 6)
    for position, parts in cuts:
        heights = jnp.exp(jax.random.uniform(jax.random.fold_in(own, position), (parts,), jnp.float32, least / len(cuts), top_value / len(cuts)))
        gain = gain * jnp.repeat(heights, dims[position] // parts).reshape([-1 if axis == position else 1 for axis in range(len(dims))])
    return gain


def normal_values(key, shape, scale, limit, split=(), dtype=jnp.bfloat16):
    values = jax.random.normal(key, shape, jnp.float32) * scale
    if len(split) > 0:
        values = block_scale(key, shape, split, -0.22, 0.18) * values
    return jnp.clip(values, min=-limit, max=limit).astype(dtype)


def heavy_noise(rng, shape, deviation, limit, cuts, heavy, dtype=jnp.bfloat16):
    values = deviation * jax.random.normal(rng, shape, jnp.float32)
    if cuts:
        values = values * block_scale(rng, shape, cuts, -0.22, 0.18)
    return jnp.clip(raised(values, jax.random.fold_in(rng, 3), *heavy), -limit, limit).astype(dtype)


def setup_inputs(seed: int = 0) -> dict:
    arg_keys = jax.random.split(jax.random.key(seed), 11)
    return {
        "pixels": draw_pixels(jax.random.fold_in(arg_keys[10], 71), 0),
        "dw_kernel": draw_dw_kernel(jax.random.fold_in(arg_keys[10], 71), 0),
        "dw_bias": normal_values(arg_keys[2], (C,), 0.5, 3.0, ((0, 4),), jnp.float32),
        "ln_gain": jnp.clip(1.0 + 0.15 * jax.random.normal(arg_keys[3], (C,), jnp.float32), 0.25, 1.75),
        "ln_bias": normal_values(arg_keys[4], (C,), 0.3, 2.0, ((0, 4),), jnp.float32),
        "w_in": normal_values(arg_keys[5], (HID, C), C ** -0.5, 0.1875, ((0, 4),)),
        "b_in": normal_values(arg_keys[6], (HID,), 0.3, 2.0, ((0, 4),)),
        "w_out": heavy_noise(arg_keys[7], (HID, C), HID ** -0.5, 0.125, ((0, 4),), (0, 1, 4, 2.0)),
        "b_out": normal_values(arg_keys[8], (C,), 0.3, 2.0, ((0, 4),), jnp.float32),
        "layer_scale": jnp.clip(jnp.exp(math.log(2.0) - 1.3862944 * jax.random.uniform(arg_keys[9], (C,), jnp.float32) ** block_scale(arg_keys[9], (C,), ((0, 4),), -0.2, 0.2)), 0.5, 2.0),
    }


def reference(pixels, dw_kernel, dw_bias, ln_gain, ln_bias, w_in, b_in, w_out, b_out, layer_scale):
    source = pixels.astype(jnp.float32)
    reach = (KS - 1) // 2
    height, width = (source.shape[0], source.shape[1])
    padded = jnp.pad(source, ((reach, reach), (reach, reach), (0, 0)))
    conv_out = jnp.zeros_like(source) + dw_bias
    for row_off in range(KS):
        for col_off in range(KS):
            conv_out = conv_out + padded[row_off:row_off + height, col_off:col_off + width, :] * dw_kernel[row_off, col_off]
    means = lax.optimization_barrier(jnp.mean(conv_out, axis=-1, keepdims=True))
    centred = conv_out - means
    spread = lax.optimization_barrier(jnp.mean(centred * centred, axis=-1, keepdims=True))
    normed = (centred * lax.rsqrt(spread + 1e-06) * ln_gain + ln_bias).astype(jnp.bfloat16)
    flat_rows = normed.reshape(-1, C).astype(jnp.float32)
    shard = HID // N_BLK
    w_in_f = w_in.astype(jnp.float32).reshape(N_BLK, shard, C)
    b_in_f = b_in.astype(jnp.float32).reshape(N_BLK, shard)
    w_out_f = w_out.astype(jnp.float32).reshape(N_BLK, shard, C)

    def add_shard(accum, items):
        w_first, b_first, w_second = items
        pre_act = jnp.dot(flat_rows, w_first.T, precision=lax.Precision.HIGHEST)
        hidden = jax.nn.gelu(pre_act + b_first, approximate=False).astype(jnp.bfloat16)
        partial_value = jnp.dot(hidden.astype(jnp.float32), w_second, precision=lax.Precision.HIGHEST).astype(jnp.bfloat16)
        partial_value = lax.optimization_barrier(partial_value)
        return (accum + partial_value.astype(jnp.float32), None)
    start_acc = jnp.zeros((flat_rows.shape[0], C), jnp.float32)
    mlp_sum = lax.scan(add_shard, start_acc, (w_in_f, b_in_f, w_out_f))[0]
    result = source + layer_scale * (mlp_sum.reshape(source.shape) + b_out)
    return result.astype(jnp.bfloat16)
```

```python
import functools
import jax
import jax.numpy as jnp
from jax import lax
from jax.experimental import pallas as pl
from jax.experimental.pallas import tpu as pltpu
from jax.sharding import Mesh, PartitionSpec as P

KS = 7


def with_halo(cells, sides, width):
    for axis, dim in sides:
        count = lax.axis_size(axis)
        ends = count - 1
        head = lax.slice_in_dim(cells, 0, width, axis=dim)
        tail = lax.slice_in_dim(cells, cells.shape[dim] - width, cells.shape[dim], axis=dim)
        cells = jnp.concatenate(
            [
                lax.ppermute(tail, axis, [(i, (i + 1) % count) for i in range(ends)]),
                cells,
                lax.ppermute(head, axis, [((i + 1) % count, i) for i in range(ends)]),
            ],
            axis=dim,
        )
    return cells


def rotated(value, shift):
    count = lax.axis_size("blk")
    return lax.ppermute(value, "blk", [(i, (i + shift) % count) for i in range(count)])


def gathered(weights):
    half = weights.shape[0] // 2
    part = half // (lax.axis_size("y") * lax.axis_size("col"))
    place = lax.axis_index("y") * lax.axis_size("col") + lax.axis_index("col")
    own = lax.dynamic_slice_in_dim(
        weights, lax.axis_index("core") * half + place * part, part, axis=0
    )
    return lax.all_gather(own, ("blk", "y", "col"), axis=0, tiled=True)


def passed(w_in, b_in, w_out):
    chans = w_in.shape[1]
    half = w_in.shape[0] // 2
    plane = lax.axis_size("y") * lax.axis_size("col")
    part = half // plane
    start = lax.axis_index("core") * half
    place = lax.axis_index("y") * lax.axis_size("col") + lax.axis_index("col")
    begin = start + place * part
    bias_row = jnp.pad(
        lax.dynamic_slice_in_dim(b_in, begin, part)[None, :], ((0, 15), (0, chans - part))
    )
    own = jnp.concatenate(
        [
            lax.dynamic_slice_in_dim(w_in, begin, part, axis=0),
            lax.dynamic_slice_in_dim(w_out, begin, part, axis=0),
            bias_row,
        ]
    )
    pieces = []
    for k in range(1, lax.axis_size("blk")):
        arrived = rotated(own, k)
        pieces.append(arrived)
        for j in range(1, plane):
            pieces.append(lax.ppermute(arrived, ("y", "col"), [(i, i ^ j) for i in range(plane)]))
    w_first = [lax.dynamic_slice_in_dim(w_in, start, half, axis=0)] + [p[:part] for p in pieces]
    w_second = [lax.dynamic_slice_in_dim(w_out, start, half, axis=0)] + [
        p[part : 2 * part] for p in pieces
    ]
    bias = [lax.dynamic_slice_in_dim(b_in, start, half)] + [p[2 * part, :part] for p in pieces]
    return jnp.concatenate(w_first), jnp.concatenate(bias), jnp.concatenate(w_second)


def collected(w_in, b_in, w_out):
    half = b_in.shape[0] // 2
    b_first = lax.all_gather(
        lax.dynamic_slice_in_dim(b_in, lax.axis_index("core") * half, half),
        "blk",
        axis=0,
        tiled=True,
    )
    return gathered(w_in), b_first, gathered(w_out)


def mlp_kernel(own_ref, peer_ref, first_ref, bias_ref, second_ref, own_out, peer_out, total):
    step = pl.program_id(0)

    @pl.when(step == 0)
    def _():
        own_out[...] = jnp.zeros_like(own_out)
        total[...] = jnp.zeros_like(total)

    bias = bias_ref[...].astype(jnp.float32)
    for rows, sums in ((peer_ref, total), (own_ref, own_out)):
        pre_act = lax.dot_general(
            rows[...], first_ref[...], (((1,), (1,)), ((), ())), preferred_element_type=jnp.float32
        )
        pre_act = pre_act + bias
        hidden = 0.5 * pre_act * (1.0 + lax.erf(pre_act * 0.7071067811865476))
        sums[...] += jnp.dot(
            hidden.astype(jnp.bfloat16), second_ref[...], preferred_element_type=jnp.float32
        )

    @pl.when(step == pl.num_programs(0) - 1)
    def _():
        peer_out[...] = total[...].astype(peer_out.dtype)


def mlp_terms(own, peer, w_first, bias, w_second):
    count, chans = own.shape
    hid = w_first.shape[0]
    tile = min(1024, hid)
    whole = pl.BlockSpec((count, chans), lambda i: (0, 0))
    return pl.pallas_call(
        mlp_kernel,
        grid=(hid // tile,),
        in_specs=[
            whole,
            whole,
            pl.BlockSpec((tile, chans), lambda i: (i, 0)),
            pl.BlockSpec((1, tile), lambda i: (0, i)),
            pl.BlockSpec((tile, chans), lambda i: (i, 0)),
        ],
        out_specs=[whole, whole],
        out_shape=[
            jax.ShapeDtypeStruct((count, chans), jnp.float32),
            jax.ShapeDtypeStruct((count, chans), jnp.bfloat16),
        ],
        scratch_shapes=[pltpu.VMEM((count, chans), jnp.float32)],
        compiler_params=pltpu.CompilerParams(vmem_limit_bytes=48 * 1024 * 1024),
        cost_estimate=pl.CostEstimate(
            flops=8 * count * chans * hid, bytes_accessed=16 * count * chans, transcendentals=0
        ),
    )(own, peer, w_first, bias, w_second)


def general(pixels, dw_kernel, dw_bias, ln_gain, ln_bias, w_in, b_in, w_out, b_out, layer_scale):
    tile_rows, tile_cols, chans = pixels.shape
    reach = (KS - 1) // 2
    blks = lax.axis_size("blk")
    plane = lax.axis_size("y") * lax.axis_size("col")
    few = plane in (1, 2, 4) and blks * plane <= 32
    w_first, b_first, w_second = (passed if few else collected)(w_in, b_in, w_out)
    padded = with_halo(pixels, ((("y", "core"), 0), ("col", 1)), reach).astype(jnp.float32)
    conv_out = jnp.zeros((tile_rows, tile_cols, chans), jnp.float32) + dw_bias
    for row_off in range(KS):
        for col_off in range(KS):
            conv_out = (
                conv_out
                + padded[row_off : row_off + tile_rows, col_off : col_off + tile_cols, :]
                * dw_kernel[row_off, col_off]
            )
    part_mean = jnp.mean(conv_out, axis=-1)
    off = conv_out - part_mean[..., None]
    part_sq = jnp.sum(off * off, axis=-1)
    stats = jnp.stack([part_mean, part_sq])
    everyone = [stats] + [rotated(stats, k) for k in range(1, blks)]
    mean = sum(s[0] for s in everyone) / blks
    sq = sum(s[1] + chans * (s[0] - mean) ** 2 for s in everyone)
    spread = sq / (chans * blks)
    normed = (
        (conv_out - mean[..., None]) * lax.rsqrt(spread + 1e-06)[..., None] * ln_gain + ln_bias
    ).astype(jnp.bfloat16)
    pixel_count = tile_rows * tile_cols
    own_px = pixel_count // blks
    flat = normed.reshape(blks, own_px, chans)
    regrouped = lax.all_to_all(flat.reshape(pixel_count, chans), "blk", split_axis=0, concat_axis=1, tiled=True)
    swap = [(0, 1), (1, 0)]
    peer = lax.ppermute(regrouped, "core", swap)
    kept, sent = mlp_terms(regrouped, peer, w_first, b_first[None, :], w_second)
    mlp = kept + lax.ppermute(sent, "core", swap).astype(jnp.float32)
    mlp = mlp.astype(jnp.bfloat16)
    summed = lax.all_to_all(mlp, "blk", split_axis=1, concat_axis=0, tiled=True)
    result = pixels.astype(jnp.float32) + layer_scale * (
        summed.astype(jnp.float32).reshape(tile_rows, tile_cols, chans) + b_out
    )
    return result.astype(jnp.bfloat16)


REACH = (KS - 1) // 2
PARTS = 4
BLOCK = 128


def fused_kernel(
    px, dwk, dw_bias, gain, beta, b_in, w_in, w_out,
    out,
    pad, taps, conv, edge, edge_in, rows_in, corner_in, edge_f, stat, norm_stat, bias,
    first, second, a_send, act, acc, p_send, p_in, r_send,
    own_sem, halo_s, halo_r, bias_s, bias_r, stat_s, stat_r,
    zown_s, zfwd_s, z_r, x_s, x_r, c_s, c_r,
    a_s, a_r, a_l, y_s, y_r, p_s, p_r, r_s, r_r, r_l,
):
    tile_rows, tile_cols, chans = px.shape
    blks = lax.axis_size("blk")
    last_row = lax.axis_size("y") * 2 - 1
    y, c, x, z = (lax.axis_index(name) for name in ("y", "core", "col", "blk"))
    row = 2 * y + c
    group_rows = tile_rows // blks
    high, wide = group_rows + 2 * REACH, tile_cols + 2 * REACH
    half = first.shape[1]
    eighth = half // 4
    part_rows = group_rows // PARTS
    part_px = part_rows * tile_cols
    part_regs = part_px * 8
    stat_blocks = part_regs // BLOCK
    full = blks * chans

    def above(extra):
        return {"y": (row - 1) // 2, "core": (row - 1) % 2, **extra}

    def below(extra):
        return {"y": (row + 1) // 2, "core": (row + 1) % 2, **extra}

    def at_z(index):
        return {"blk": index}

    has_up, has_down = row > 0, row < last_row
    side = {"col": 1 - x}
    sibling = {"core": 1 - c}
    partner = {"y": 1 - y}

    def when(cond, act_fn):
        if cond is None:
            act_fn()
        else:
            pl.when(cond)(act_fn)

    sent = []

    def send(make, cond=None):
        when(cond, lambda: make().start())
        sent.append((make, cond))

    def remote(src, dst, send_sem, recv_sem, device):
        return pltpu.make_async_remote_copy(
            src_ref=src, dst_ref=dst, send_sem=send_sem, recv_sem=recv_sem,
            device_id=device, device_id_type=pl.DeviceIdType.MESH,
        )

    def arrived(dst, send_sem, recv_sem, device):
        remote(dst, dst, send_sem, recv_sem, device).wait_recv()

    barrier = pltpu.get_barrier_semaphore()

    def greet(device):
        pl.semaphore_signal(barrier, inc=1, device_id=device, device_id_type=pl.DeviceIdType.MESH)

    for device in (side, sibling, partner):
        greet(device)
    for step in range(1, blks):
        greet(at_z((z + step) % blks))

    @pl.when(has_up)
    def _():
        greet(above({}))
        greet(above(side))

    @pl.when(has_down)
    def _():
        greet(below({}))
        greet(below(side))

    pl.semaphore_wait(barrier, 2 + blks + 2 * jnp.where(has_up, 1, 0) + 2 * jnp.where(has_down, 1, 0))

    send(lambda: remote(px.at[pl.ds(0, REACH)], rows_in.at[1], halo_s.at[0], halo_r.at[1], above({})), has_up)
    send(
        lambda: remote(
            px.at[pl.ds(tile_rows - REACH, REACH)], rows_in.at[0], halo_s.at[1], halo_r.at[0], below({})
        ),
        has_down,
    )

    start = pl.multiple_of(y * half, half)
    mine = pl.multiple_of(x * (half // 2) + c * eighth, eighth)
    across = pl.multiple_of((1 - x) * (half // 2) + c * eighth, eighth)
    weights = ((w_in, first), (w_out, second))
    for k, (src, dst) in enumerate(weights):
        piece = lambda src=src: src.at[pl.ds(pl.multiple_of(start + mine, eighth), eighth)]
        for way, cond, step in ((0, z < blks - 1, 1), (1, z > 0, -1)):
            send(
                lambda k=k, way=way, step=step, piece=piece, dst=dst: remote(
                    piece(), dst.at[z, pl.ds(mine, eighth)], zown_s.at[k, way], z_r.at[k, z], at_z(z + step)
                ),
                cond,
            )
    own = [
        pltpu.make_async_copy(src.at[pl.ds(start, half)], dst.at[z], own_sem.at[k])
        for k, (src, dst) in enumerate(weights)
    ]
    for copy in own:
        copy.start()

    bias[z] = jnp.broadcast_to(b_in[:, pl.ds(start, half)], (8, half))
    for step in range(1, blks):
        send(
            lambda step=step: remote(
                bias.at[z], bias.at[z], bias_s.at[step], bias_r.at[z], at_z((z + step) % blks)
            )
        )

    def body(i, _):
        pad[pl.ds(pl.multiple_of(i * 8 * wide, 8), 8 * wide), :] = jnp.zeros((8 * wide, 128), jnp.float32)
        return 0

    lax.fori_loop(0, high, body, 0)
    edge_f[...] = jnp.zeros_like(edge_f)

    def put_row(values, group, line):
        for tile in range(2):
            pad[pl.ds((line * wide + REACH) * 8 + 4 * tile + group, tile_cols, stride=8), :] = values[
                :, tile * 128 : (tile + 1) * 128
            ]

    for group in range(blks):
        low = REACH if group == 0 else 0
        top = high - (REACH if group == blks - 1 else 0)

        def body(line, _, group=group):
            put_row(px[group * group_rows + line - REACH].astype(jnp.float32), group, line)
            return 0

        lax.fori_loop(low, top, body, 0)

    take = jnp.where(x == 0, tile_cols, REACH)
    for j in range(REACH):
        for tile in range(2):
            for group in range(blks):
                edge[j, group * group_rows : (group + 1) * group_rows, tile * 128 : (tile + 1) * 128] = pad[
                    pl.ds((REACH * wide + take + j) * 8 + 4 * tile + group, group_rows, stride=8 * wide), :
                ].astype(jnp.bfloat16)
    send(lambda: remote(edge, edge_in, halo_s.at[2], halo_r.at[2], side))
    send(
        lambda: remote(edge.at[:, pl.ds(0, 16)], corner_in.at[1], halo_s.at[3], halo_r.at[4], above(side)), has_up
    )
    send(
        lambda: remote(
            edge.at[:, pl.ds(tile_rows - 16, 16)], corner_in.at[0], halo_s.at[4], halo_r.at[3], below(side)
        ),
        has_down,
    )

    for i in range(KS):
        for tile in range(2):
            for group in range(4):
                taps[pl.ds(i * KS * 8 + 4 * tile + group, KS, stride=8), :] = dwk[
                    i, :, tile * 128 : (tile + 1) * 128
                ]
    upper = lax.broadcasted_iota(jnp.int32, (8, 128), 0) < 4

    def tiled(ref):
        return jnp.where(
            upper, jnp.broadcast_to(ref[:, 0:128], (8, 128)), jnp.broadcast_to(ref[:, 128:256], (8, 128))
        )

    @pl.when(has_up)
    def _():
        arrived(rows_in.at[0], halo_s.at[0], halo_r.at[0], above({}))
        for i in range(REACH):
            put_row(rows_in[0, i].astype(jnp.float32), 0, i)

    @pl.when(has_down)
    def _():
        arrived(rows_in.at[1], halo_s.at[1], halo_r.at[1], below({}))
        for i in range(REACH):
            put_row(rows_in[1, i].astype(jnp.float32), blks - 1, high - REACH + i)

    arrived(edge_in, halo_s.at[2], halo_r.at[2], side)
    for j in range(REACH):
        for tile in range(2):
            edge_f[j, tile, REACH : REACH + tile_rows, :] = edge_in[
                j, :, tile * 128 : (tile + 1) * 128
            ].astype(jnp.float32)

    @pl.when(has_up)
    def _():
        arrived(corner_in.at[0], halo_s.at[3], halo_r.at[3], above(side))
        for j in range(REACH):
            for tile in range(2):
                edge_f[j, tile, 0:REACH, :] = corner_in[0, j, :, tile * 128 : (tile + 1) * 128].astype(
                    jnp.float32
                )[16 - REACH :]

    @pl.when(has_down)
    def _():
        arrived(corner_in.at[1], halo_s.at[4], halo_r.at[4], below(side))
        for j in range(REACH):
            for tile in range(2):
                edge_f[j, tile, REACH + tile_rows : 2 * REACH + tile_rows, :] = corner_in[
                    1, j, :, tile * 128 : (tile + 1) * 128
                ].astype(jnp.float32)[:REACH]

    place = jnp.where(x == 0, tile_cols + REACH, 0)
    for j in range(REACH):
        for tile in range(2):
            for group in range(blks):
                pad[pl.ds((place + j) * 8 + 4 * tile + group, high, stride=8 * wide), :] = edge_f[
                    j, tile, group * group_rows : group * group_rows + high, :
                ]

    def convolve(part):
        def body(i, _):
            line = part * part_rows + i // (tile_cols // 8)
            col = (i % (tile_cols // 8)) * 8
            total = jnp.broadcast_to(tiled(dw_bias)[None], (8, 8, 128))
            for up in range(KS):
                begin = pl.multiple_of(((line + up) * wide + col) * 8, 8)
                cells = pad[pl.ds(begin, 8 * (7 + KS)), :].reshape(7 + KS, 8, 128)
                for j in range(KS):
                    weight = taps[(up * KS + j) * 8 : (up * KS + j + 1) * 8, :]
                    total = total + cells[j : j + 8] * weight[None]
            conv[pl.ds(pl.multiple_of((line * tile_cols + col) * 8, 64), 64), :] = total.reshape(64, 128)
            return 0

        lax.fori_loop(0, part_px // 8, body, 0)

    def both_tiles(values):
        return values + pltpu.roll(values, 4, 1)

    def measure(part):
        def body(b, _):
            cells = conv[pl.ds(pl.multiple_of(part * part_regs + b * BLOCK, BLOCK), BLOCK), :].reshape(
                BLOCK // 8, 8, 128
            )
            sums = jnp.broadcast_to(jnp.sum(cells, axis=2, keepdims=True), cells.shape)
            mean = both_tiles(sums) * (1.0 / chans)
            off = cells - mean
            squares = both_tiles(jnp.broadcast_to(jnp.sum(off * off, axis=2, keepdims=True), cells.shape))
            lane = lax.broadcasted_iota(jnp.int32, cells.shape, 2)
            turned = jnp.where(lane == 0, mean, squares).reshape(BLOCK, 128).T
            stat[part, z, 0, pl.ds(b, 1), :] = turned[0:1]
            stat[part, z, 1, pl.ds(b, 1), :] = turned[1:2]
            return 0

        lax.fori_loop(0, stat_blocks, body, 0)
        for step in range(1, blks):
            send(
                lambda step=step: remote(
                    stat.at[part, z], stat.at[part, z], stat_s.at[part, step], stat_r.at[part, z],
                    at_z((z + step) % blks),
                )
            )

    def columns(index):
        return pl.ds(pl.multiple_of(index * chans, chans), chans)

    def normalize(part):
        for step in range(1, blks):
            other = (z + step) % blks
            arrived(stat.at[part, other], stat_s.at[part, step], stat_r.at[part, other], at_z(other))
        mean = sum(stat[part, o, 0] for o in range(blks)) / blks
        spread = sum(stat[part, o, 1] + chans * (stat[part, o, 0] - mean) ** 2 for o in range(blks)) / full
        norm_stat[0] = mean
        norm_stat[1] = lax.rsqrt(spread + 1e-06)

        def body(b, _):
            where = pl.ds(pl.multiple_of(part * part_regs + b * BLOCK, BLOCK), BLOCK)
            cells = conv[where, :].reshape(BLOCK // 8, 8, 128)
            means, scales = (
                jnp.broadcast_to(norm_stat[k, pl.ds(b, 1), :], (BLOCK, 128)).T.reshape(BLOCK // 8, 8, 128)
                for k in range(2)
            )
            normed = (cells - means) * scales * tiled(gain)[None] + tiled(beta)[None]
            conv[where, :] = normed.reshape(BLOCK, 128)
            return 0

        lax.fori_loop(0, stat_blocks, body, 0)
        for group in range(blks):
            for tile in range(2):
                a_send[part, group, :, tile * 128 : (tile + 1) * 128] = conv[
                    pl.ds(part * part_regs + 4 * tile + group, part_px, stride=8), :
                ].astype(jnp.bfloat16)
        for step in range(1, blks):
            send(
                lambda step=step: remote(
                    a_send.at[part, (z + step) % blks], act.at[part, pl.ds(0, part_px), columns(z)],
                    a_s.at[part, step], a_r.at[part, z], at_z((z + step) % blks),
                )
            )
        pltpu.make_async_copy(
            a_send.at[part, z], act.at[part, pl.ds(0, part_px), columns(z)], a_l.at[part]
        ).start()

    def swap_rows(part):
        for step in range(1, blks):
            other = (z + step) % blks
            arrived(
                act.at[part, pl.ds(0, part_px), columns(other)], a_s.at[part, step], a_r.at[part, other], at_z(other)
            )
        pltpu.make_async_copy(
            a_send.at[part, z], act.at[part, pl.ds(0, part_px), columns(z)], a_l.at[part]
        ).wait()
        send(
            lambda: remote(
                act.at[part, pl.ds(0, part_px)], act.at[part, pl.ds(part_px, part_px)],
                y_s.at[part], y_r.at[part], partner,
            )
        )

    def both_ways(dist):
        return ((z >= dist, lambda: z - dist, z < blks - 1, 1), (z + dist < blks, lambda: z + dist, z > 0, -1))

    def relay(dist, k):
        block = weights[k][1]
        for cond, origin, more, step in both_ways(dist):
            spot = lambda origin=origin: block.at[origin(), pl.ds(mine, eighth)]
            when(
                cond,
                lambda spot=spot, origin=origin: arrived(spot(), zown_s.at[k, 0], z_r.at[k, origin()], side),
            )
            if dist < blks - 1:
                send(
                    lambda spot=spot, origin=origin, step=step: remote(
                        spot(), spot(), zfwd_s.at[k, origin()], z_r.at[k, origin()], at_z(z + step)
                    ),
                    cond & more,
                )
            send(
                lambda spot=spot, origin=origin: remote(
                    spot(), spot(), x_s.at[k, origin()], x_r.at[k, origin()], side
                ),
                cond,
            )
            send(
                lambda spot=spot, origin=origin: remote(
                    spot(), spot(), c_s.at[k, 0, origin()], c_r.at[k, 0, origin()], sibling
                ),
                cond,
            )

    def share(dist, k):
        block = weights[k][1]
        for cond, origin, _, _ in both_ways(dist):
            spot = lambda origin=origin: block.at[origin(), pl.ds(across, eighth)]
            when(
                cond,
                lambda spot=spot, origin=origin: arrived(
                    spot(), x_s.at[k, origin()], x_r.at[k, origin()], side
                ),
            )
            send(
                lambda spot=spot, origin=origin: remote(
                    spot(), spot(), c_s.at[k, 1, origin()], c_r.at[k, 1, origin()], sibling
                ),
                cond,
            )

    def ready():
        for copy in own:
            copy.wait()
        for step in range(1, blks):
            other = (z + step) % blks
            arrived(bias.at[other], bias_s.at[step], bias_r.at[other], at_z(other))
            for k in range(2):
                for n, column in ((0, x), (1, 1 - x)):
                    begin = pl.multiple_of(column * (half // 2) + (1 - c) * eighth, eighth)
                    arrived(
                        weights[k][1].at[other, pl.ds(begin, eighth)],
                        c_s.at[k, n, other], c_r.at[k, n, other], sibling,
                    )

    def feed(part):
        arrived(act.at[part, pl.ds(part_px, part_px)], y_s.at[part], y_r.at[part], partner)

        def body(o, _):
            pre_act = lax.dot_general(
                act[part], first[o], (((1,), (1,)), ((), ())), preferred_element_type=jnp.float32
            )
            pre_act = pre_act + bias[o, 0:1, :]
            hidden = 0.5 * pre_act * (1.0 + lax.erf(pre_act * 0.7071067811865476))
            term = jnp.dot(hidden.astype(jnp.bfloat16), second[o], preferred_element_type=jnp.float32)

            @pl.when(o == 0)
            def _():
                acc[part] = term

            @pl.when(o > 0)
            def _():
                acc[part] += term

            return 0

        lax.fori_loop(0, blks, body, 0)
        p_send[part] = acc[part, part_px:, :].astype(jnp.bfloat16)
        send(lambda: remote(p_send.at[part], p_in.at[part], p_s.at[part], p_r.at[part], partner))

    def result_rows(owner, part):
        return out.at[pl.ds(pl.multiple_of(owner * (part_px * PARTS) + part * part_px, part_px), part_px)]

    def give_back(part):
        arrived(p_in.at[part], p_s.at[part], p_r.at[part], partner)
        r_send[part] = (acc[part, :part_px, :] + p_in[part].astype(jnp.float32)).astype(jnp.bfloat16)
        for step in range(1, blks):
            send(
                lambda step=step: remote(
                    r_send.at[part, :, columns((z + step) % blks)], result_rows(z, part),
                    r_s.at[part, step], r_r.at[part, z], at_z((z + step) % blks),
                )
            )
        pltpu.make_async_copy(r_send.at[part, :, columns(z)], result_rows(z, part), r_l.at[part]).start()

    def collect(part):
        for step in range(1, blks):
            other = (z + step) % blks
            arrived(result_rows(other, part), r_s.at[part, step], r_r.at[part, other], at_z(other))
        pltpu.make_async_copy(r_send.at[part, :, columns(z)], result_rows(z, part), r_l.at[part]).wait()

    convolve(0)
    measure(0)
    relay(1, 0)
    convolve(1)
    measure(1)
    normalize(0)
    relay(1, 1)
    share(1, 0)
    convolve(2)
    measure(2)
    normalize(1)
    relay(2, 0)
    share(1, 1)
    convolve(3)
    measure(3)
    normalize(2)
    normalize(3)
    relay(2, 1)
    share(2, 0)
    swap_rows(0)
    relay(3, 0)
    share(2, 1)
    swap_rows(1)
    relay(3, 1)
    share(3, 0)
    swap_rows(2)
    share(3, 1)
    ready()
    feed(0)
    swap_rows(3)
    feed(1)
    give_back(0)
    feed(2)
    give_back(1)
    feed(3)
    give_back(2)
    give_back(3)
    for part in range(PARTS):
        collect(part)
    for make, cond in sent:
        when(cond, lambda make=make: make().wait_send())


def fused(pixels, dw_kernel, dw_bias, ln_gain, ln_bias, w_in, b_in, w_out, b_out, layer_scale):
    tile_rows, tile_cols, chans = pixels.shape
    blks = lax.axis_size("blk")
    full = blks * chans
    half = w_in.shape[0] // 2
    group_rows = tile_rows // blks
    px = group_rows * tile_cols
    part_px = px // PARTS
    high, wide = group_rows + 2 * REACH, tile_cols + 2 * REACH
    vmem, dma = pltpu.VMEM, pltpu.SemaphoreType.DMA
    here = pl.BlockSpec(memory_space=pltpu.VMEM)
    anywhere = pl.BlockSpec(memory_space=pl.ANY)
    bf16, f32 = jnp.bfloat16, jnp.float32
    summed = pl.pallas_call(
        fused_kernel,
        in_specs=[here] * 6 + [anywhere] * 2,
        out_specs=anywhere,
        out_shape=jax.ShapeDtypeStruct((tile_rows * tile_cols, chans), bf16),
        scratch_shapes=[
            vmem((high * wide * 8, 128), f32),
            vmem((KS * KS * 8, 128), f32),
            vmem((px * 8, 128), f32),
            vmem((REACH, tile_rows, chans), bf16),
            vmem((REACH, tile_rows, chans), bf16),
            vmem((2, REACH, tile_cols, chans), bf16),
            vmem((2, REACH, 16, chans), bf16),
            vmem((REACH, 2, tile_rows + 8, 128), f32),
            vmem((PARTS, blks, 2, 8, 128), f32),
            vmem((2, 8, 128), f32),
            vmem((blks, 8, half), f32),
            vmem((blks, half, full), bf16),
            vmem((blks, half, full), bf16),
            vmem((PARTS, blks, part_px, chans), bf16),
            vmem((PARTS, 2 * part_px, full), bf16),
            vmem((PARTS, 2 * part_px, full), f32),
            vmem((PARTS, part_px, full), bf16),
            vmem((PARTS, part_px, full), bf16),
            vmem((PARTS, part_px, full), bf16),
            dma((2,)), dma((5,)), dma((5,)), dma((blks,)), dma((blks,)), dma((PARTS, blks)), dma((PARTS, blks)),
            dma((2, 2)), dma((2, blks)), dma((2, blks)), dma((2, blks)), dma((2, blks)),
            dma((2, 2, blks)), dma((2, 2, blks)),
            dma((PARTS, blks)), dma((PARTS, blks)), dma((PARTS,)),
            dma((PARTS,)), dma((PARTS,)), dma((PARTS,)), dma((PARTS,)),
            dma((PARTS, blks)), dma((PARTS, blks)), dma((PARTS,)),
        ],
        compiler_params=pltpu.CompilerParams(
            collective_id=0, has_side_effects=True, vmem_limit_bytes=48 * 1024 * 1024
        ),
    )(
        pixels, dw_kernel, dw_bias[None, :], ln_gain[None, :], ln_bias[None, :],
        b_in.astype(f32)[None, :], w_in, w_out,
    )
    result = pixels.astype(f32) + layer_scale * (
        summed.astype(f32).reshape(tile_rows, tile_cols, chans) + b_out
    )
    return result.astype(bf16)


def shards(pixels, *params):
    tile_rows, tile_cols, chans = pixels.shape
    blks = lax.axis_size("blk")
    fits = (
        (lax.axis_size("y"), lax.axis_size("col"), blks, chans) == (2, 2, 4, 256)
        and tile_cols % 16 == 0
        and tile_rows % (4 * blks) == 0
        and tile_rows * tile_cols == blks * PARTS * BLOCK
        and params[4].shape[0] % 1024 == 0
    )
    return (fused if fits else general)(pixels, *params)


def solution(mesh):
    row, col, blk = (mesh.shape[name] for name in ("row", "col", "blk"))
    split = Mesh(mesh.devices.reshape(row // 2, 2, col, blk), ("y", "core", "col", "blk"))
    placed = (
        P(("y", "core"), "col", "blk"),
        P(None, None, "blk"),
        P("blk"),
        P("blk"),
        P("blk"),
        P("blk", None),
        P("blk"),
        P("blk", None),
        P("blk"),
        P("blk"),
    )
    return jax.shard_map(
        shards, mesh=split, in_specs=placed, out_specs=P(("y", "core"), "col", "blk"), check_vma=False
    )
```

```python
import functools
import jax
import jax.numpy as jnp
from jax import lax
from jax.experimental import pallas as pl
from jax.experimental.pallas import tpu as pltpu
from jax.sharding import Mesh, PartitionSpec as P

KS = 7


def with_halo(cells, sides, width):
    for axis, dim in sides:
        count = lax.axis_size(axis)
        ends = count - 1
        head = lax.slice_in_dim(cells, 0, width, axis=dim)
        tail = lax.slice_in_dim(cells, cells.shape[dim] - width, cells.shape[dim], axis=dim)
        cells = jnp.concatenate(
            [
                lax.ppermute(tail, axis, [(i, (i + 1) % count) for i in range(ends)]),
                cells,
                lax.ppermute(head, axis, [((i + 1) % count, i) for i in range(ends)]),
            ],
            axis=dim,
        )
    return cells


def rotated(value, shift):
    count = lax.axis_size("blk")
    return lax.ppermute(value, "blk", [(i, (i + shift) % count) for i in range(count)])


def gathered(weights):
    half = weights.shape[0] // 2
    part = half // (lax.axis_size("y") * lax.axis_size("col"))
    place = lax.axis_index("y") * lax.axis_size("col") + lax.axis_index("col")
    own = lax.dynamic_slice_in_dim(
        weights, lax.axis_index("core") * half + place * part, part, axis=0
    )
    return lax.all_gather(own, ("blk", "y", "col"), axis=0, tiled=True)


def passed(w_in, b_in, w_out):
    chans = w_in.shape[1]
    half = w_in.shape[0] // 2
    plane = lax.axis_size("y") * lax.axis_size("col")
    part = half // plane
    start = lax.axis_index("core") * half
    place = lax.axis_index("y") * lax.axis_size("col") + lax.axis_index("col")
    begin = start + place * part
    bias_row = jnp.pad(
        lax.dynamic_slice_in_dim(b_in, begin, part)[None, :], ((0, 15), (0, chans - part))
    )
    own = jnp.concatenate(
        [
            lax.dynamic_slice_in_dim(w_in, begin, part, axis=0),
            lax.dynamic_slice_in_dim(w_out, begin, part, axis=0),
            bias_row,
        ]
    )
    pieces = []
    for k in range(1, lax.axis_size("blk")):
        arrived = rotated(own, k)
        pieces.append(arrived)
        for j in range(1, plane):
            pieces.append(lax.ppermute(arrived, ("y", "col"), [(i, i ^ j) for i in range(plane)]))
    w_first = [lax.dynamic_slice_in_dim(w_in, start, half, axis=0)] + [p[:part] for p in pieces]
    w_second = [lax.dynamic_slice_in_dim(w_out, start, half, axis=0)] + [
        p[part : 2 * part] for p in pieces
    ]
    bias = [lax.dynamic_slice_in_dim(b_in, start, half)] + [p[2 * part, :part] for p in pieces]
    return jnp.concatenate(w_first), jnp.concatenate(bias), jnp.concatenate(w_second)


def collected(w_in, b_in, w_out):
    half = b_in.shape[0] // 2
    b_first = lax.all_gather(
        lax.dynamic_slice_in_dim(b_in, lax.axis_index("core") * half, half),
        "blk",
        axis=0,
        tiled=True,
    )
    return gathered(w_in), b_first, gathered(w_out)


def mlp_kernel(own_ref, peer_ref, first_ref, bias_ref, second_ref, own_out, peer_out, total):
    step = pl.program_id(0)

    @pl.when(step == 0)
    def _():
        own_out[...] = jnp.zeros_like(own_out)
        total[...] = jnp.zeros_like(total)

    bias = bias_ref[...].astype(jnp.float32)
    for rows, sums in ((peer_ref, total), (own_ref, own_out)):
        pre_act = lax.dot_general(
            rows[...], first_ref[...], (((1,), (1,)), ((), ())), preferred_element_type=jnp.float32
        )
        pre_act = pre_act + bias
        hidden = 0.5 * pre_act * (1.0 + lax.erf(pre_act * 0.7071067811865476))
        sums[...] += jnp.dot(
            hidden.astype(jnp.bfloat16), second_ref[...], preferred_element_type=jnp.float32
        )

    @pl.when(step == pl.num_programs(0) - 1)
    def _():
        peer_out[...] = total[...].astype(peer_out.dtype)


def mlp_terms(own, peer, w_first, bias, w_second):
    count, chans = own.shape
    hid = w_first.shape[0]
    tile = min(1024, hid)
    whole = pl.BlockSpec((count, chans), lambda i: (0, 0))
    return pl.pallas_call(
        mlp_kernel,
        grid=(hid // tile,),
        in_specs=[
            whole,
            whole,
            pl.BlockSpec((tile, chans), lambda i: (i, 0)),
            pl.BlockSpec((1, tile), lambda i: (0, i)),
            pl.BlockSpec((tile, chans), lambda i: (i, 0)),
        ],
        out_specs=[whole, whole],
        out_shape=[
            jax.ShapeDtypeStruct((count, chans), jnp.float32),
            jax.ShapeDtypeStruct((count, chans), jnp.bfloat16),
        ],
        scratch_shapes=[pltpu.VMEM((count, chans), jnp.float32)],
        compiler_params=pltpu.CompilerParams(vmem_limit_bytes=48 * 1024 * 1024),
        cost_estimate=pl.CostEstimate(
            flops=8 * count * chans * hid, bytes_accessed=16 * count * chans, transcendentals=0
        ),
    )(own, peer, w_first, bias, w_second)


def general(pixels, dw_kernel, dw_bias, ln_gain, ln_bias, w_in, b_in, w_out, b_out, layer_scale):
    tile_rows, tile_cols, chans = pixels.shape
    reach = (KS - 1) // 2
    blks = lax.axis_size("blk")
    plane = lax.axis_size("y") * lax.axis_size("col")
    few = plane in (1, 2, 4) and blks * plane <= 32
    w_first, b_first, w_second = (passed if few else collected)(w_in, b_in, w_out)
    padded = with_halo(pixels, ((("y", "core"), 0), ("col", 1)), reach).astype(jnp.float32)
    conv_out = jnp.zeros((tile_rows, tile_cols, chans), jnp.float32) + dw_bias
    for row_off in range(KS):
        for col_off in range(KS):
            conv_out = (
                conv_out
                + padded[row_off : row_off + tile_rows, col_off : col_off + tile_cols, :]
                * dw_kernel[row_off, col_off]
            )
    part_mean = jnp.mean(conv_out, axis=-1)
    off = conv_out - part_mean[..., None]
    part_sq = jnp.sum(off * off, axis=-1)
    stats = jnp.stack([part_mean, part_sq])
    everyone = [stats] + [rotated(stats, k) for k in range(1, blks)]
    mean = sum(s[0] for s in everyone) / blks
    sq = sum(s[1] + chans * (s[0] - mean) ** 2 for s in everyone)
    spread = sq / (chans * blks)
    normed = (
        (conv_out - mean[..., None]) * lax.rsqrt(spread + 1e-06)[..., None] * ln_gain + ln_bias
    ).astype(jnp.bfloat16)
    pixel_count = tile_rows * tile_cols
    own_px = pixel_count // blks
    flat = normed.reshape(blks, own_px, chans)
    regrouped = lax.all_to_all(flat.reshape(pixel_count, chans), "blk", split_axis=0, concat_axis=1, tiled=True)
    swap = [(0, 1), (1, 0)]
    peer = lax.ppermute(regrouped, "core", swap)
    kept, sent = mlp_terms(regrouped, peer, w_first, b_first[None, :], w_second)
    mlp = kept + lax.ppermute(sent, "core", swap).astype(jnp.float32)
    mlp = mlp.astype(jnp.bfloat16)
    summed = lax.all_to_all(mlp, "blk", split_axis=1, concat_axis=0, tiled=True)
    result = pixels.astype(jnp.float32) + layer_scale * (
        summed.astype(jnp.float32).reshape(tile_rows, tile_cols, chans) + b_out
    )
    return result.astype(jnp.bfloat16)


REACH = (KS - 1) // 2
PARTS = 4
GROUPS = 8
BLOCK = 128
STATS = 4


def fused_kernel(
    px_hbm, dwk_hbm, dw_bias_hbm, gain_hbm, beta_hbm, b_in_hbm, w_in, w_out,
    out,
    px, dwk, dw_bias, gain, beta, b_in, b_wide, load_sem,
    pad, taps, conv, edge, edge_in, rows_in, corner_in, edge_f, stat, norm_stat, bias,
    first, second, a_send, act, acc, p_send, p_in, r_send,
    own_sem, halo_s, halo_r, bias_s, bias_r, stat_s, stat_r,
    zown_s, zfwd_s, z_r, x_s, x_r, c_s, c_r,
    a_s, a_r, a_l, y_s, y_r, p_s, p_r, r_s, r_r, r_l,
):
    tile_rows, tile_cols, chans = px.shape
    blks = lax.axis_size("blk")
    last_row = lax.axis_size("y") * 2 - 1
    y, c, x, z = (lax.axis_index(name) for name in ("y", "core", "col", "blk"))
    row = 2 * y + c
    lines = tile_rows // GROUPS
    high, wide = lines + 2 * REACH, tile_cols + 2 * REACH
    half = first.shape[1]
    eighth = half // 4
    per_blk = GROUPS // blks
    part_rows = lines // PARTS
    group_px = part_rows * tile_cols
    part_px = per_blk * group_px
    part_regs = group_px * GROUPS
    stat_blocks = part_regs // BLOCK
    full = blks * chans

    def above(extra):
        return {"y": (row - 1) // 2, "core": (row - 1) % 2, **extra}

    def below(extra):
        return {"y": (row + 1) // 2, "core": (row + 1) % 2, **extra}

    def at_z(index):
        return {"blk": index}

    has_up, has_down = row > 0, row < last_row
    side = {"col": 1 - x}
    sibling = {"core": 1 - c}
    partner = {"y": 1 - y}

    def when(cond, act_fn):
        if cond is None:
            act_fn()
        else:
            pl.when(cond)(act_fn)

    sent = []

    def send(make, cond=None):
        when(cond, lambda: make().start())
        sent.append((make, cond))

    def remote(src, dst, send_sem, recv_sem, device):
        return pltpu.make_async_remote_copy(
            src_ref=src, dst_ref=dst, send_sem=send_sem, recv_sem=recv_sem,
            device_id=device, device_id_type=pl.DeviceIdType.MESH,
        )

    def arrived(dst, send_sem, recv_sem, device):
        remote(dst, dst, send_sem, recv_sem, device).wait_recv()

    loads = [
        pltpu.make_async_copy(src, dst, load_sem.at[k])
        for k, (src, dst) in enumerate(
            ((px_hbm, px), (dwk_hbm, dwk), (dw_bias_hbm, dw_bias), (gain_hbm, gain), (beta_hbm, beta), (b_in_hbm, b_in))
        )
    ]
    for copy in loads:
        copy.start()

    barrier = pltpu.get_barrier_semaphore()

    def greet(device):
        pl.semaphore_signal(barrier, inc=1, device_id=device, device_id_type=pl.DeviceIdType.MESH)

    for device in (side, sibling, partner):
        greet(device)
    for step in range(1, blks):
        greet(at_z((z + step) % blks))

    @pl.when(has_up)
    def _():
        greet(above({}))
        greet(above(side))

    @pl.when(has_down)
    def _():
        greet(below({}))
        greet(below(side))

    pl.semaphore_wait(barrier, 2 + blks + 2 * jnp.where(has_up, 1, 0) + 2 * jnp.where(has_down, 1, 0))

    send(lambda: remote(px_hbm.at[pl.ds(0, REACH)], rows_in.at[1], halo_s.at[0], halo_r.at[1], above({})), has_up)
    send(
        lambda: remote(
            px_hbm.at[pl.ds(tile_rows - REACH, REACH)], rows_in.at[0], halo_s.at[1], halo_r.at[0], below({})
        ),
        has_down,
    )

    start = pl.multiple_of(y * half, half)
    mine = pl.multiple_of(x * (half // 2) + c * eighth, eighth)
    across = pl.multiple_of((1 - x) * (half // 2) + c * eighth, eighth)
    weights = ((w_in, first), (w_out, second))
    for k, (src, dst) in enumerate(weights):
        piece = lambda src=src: src.at[pl.ds(pl.multiple_of(start + mine, eighth), eighth)]
        for way, cond, step in ((0, z < blks - 1, 1), (1, z > 0, -1)):
            send(
                lambda k=k, way=way, step=step, piece=piece, dst=dst: remote(
                    piece(), dst.at[z, pl.ds(mine, eighth)], zown_s.at[k, way], z_r.at[k, z], at_z(z + step)
                ),
                cond,
            )
    own = [
        pltpu.make_async_copy(src.at[pl.ds(start, half)], dst.at[z], own_sem.at[k])
        for k, (src, dst) in enumerate(weights)
    ]
    for copy in own:
        copy.start()

    def body(i, _):
        pad[pl.ds(pl.multiple_of(i * 8 * wide, 8), 8 * wide), :] = jnp.zeros((8 * wide, 128), jnp.float32)
        return 0

    lax.fori_loop(0, 2 * high, body, 0)
    for copy in loads:
        copy.wait()

    def spot_of(tile, line, col, group):
        return ((tile * high + line) * wide + col) * GROUPS + group

    def put_row(values, group, line):
        for tile in range(2):
            pad[pl.ds(spot_of(tile, line, REACH, group), tile_cols, stride=GROUPS), :] = values[
                :, tile * 128 : (tile + 1) * 128
            ]

    for group in range(GROUPS):
        low = REACH if group == 0 else 0
        top = high - (REACH if group == GROUPS - 1 else 0)

        def body(line, _, group=group):
            put_row(px[group * lines + line - REACH].astype(jnp.float32), group, line)
            return 0

        lax.fori_loop(low, top, body, 0)

    take = jnp.where(x == 0, tile_cols, REACH)
    for j in range(REACH):
        for tile in range(2):
            for group in range(GROUPS):
                edge_f[j, tile, group * lines : (group + 1) * lines, :] = pad[
                    pl.ds(spot_of(tile, REACH, take + j, group), lines, stride=GROUPS * wide), :
                ]
            edge[j, :, tile * 128 : (tile + 1) * 128] = edge_f[j, tile, 0:tile_rows, :].astype(jnp.bfloat16)
    send(lambda: remote(edge, edge_in, halo_s.at[2], halo_r.at[2], side))
    send(
        lambda: remote(edge.at[:, pl.ds(0, 16)], corner_in.at[1], halo_s.at[3], halo_r.at[4], above(side)), has_up
    )
    send(
        lambda: remote(
            edge.at[:, pl.ds(tile_rows - 16, 16)], corner_in.at[0], halo_s.at[4], halo_r.at[3], below(side)
        ),
        has_down,
    )

    b_wide[...] = b_in[...].astype(jnp.float32)
    share_rows = half // 128
    for k in range(share_rows):
        bias[z, :, k * 128 : (k + 1) * 128] = jnp.broadcast_to(b_wide[pl.ds(y * share_rows + k, 1), :], (8, 128))
    for step in range(1, blks):
        send(
            lambda step=step: remote(
                bias.at[z], bias.at[z], bias_s.at[step], bias_r.at[z], at_z((z + step) % blks)
            )
        )
    edge_f[...] = jnp.zeros_like(edge_f)

    def spread(ref, tile):
        return jnp.broadcast_to(ref[:, tile * 128 : (tile + 1) * 128], (GROUPS, 128))

    for tile in range(2):
        for i in range(KS):
            for j in range(KS):
                at = ((tile * KS + i) * KS + j) * GROUPS
                taps[at : at + GROUPS, :] = jnp.broadcast_to(
                    dwk[i, j : j + 1, tile * 128 : (tile + 1) * 128], (GROUPS, 128)
                )

    @pl.when(has_up)
    def _():
        arrived(rows_in.at[0], halo_s.at[0], halo_r.at[0], above({}))
        for i in range(REACH):
            put_row(rows_in[0, i].astype(jnp.float32), 0, i)

    @pl.when(has_down)
    def _():
        arrived(rows_in.at[1], halo_s.at[1], halo_r.at[1], below({}))
        for i in range(REACH):
            put_row(rows_in[1, i].astype(jnp.float32), GROUPS - 1, high - REACH + i)

    arrived(edge_in, halo_s.at[2], halo_r.at[2], side)
    for j in range(REACH):
        for tile in range(2):
            edge_f[j, tile, REACH : REACH + tile_rows, :] = edge_in[
                j, :, tile * 128 : (tile + 1) * 128
            ].astype(jnp.float32)

    @pl.when(has_up)
    def _():
        arrived(corner_in.at[0], halo_s.at[3], halo_r.at[3], above(side))
        for j in range(REACH):
            for tile in range(2):
                edge_f[j, tile, 0:REACH, :] = corner_in[0, j, :, tile * 128 : (tile + 1) * 128].astype(
                    jnp.float32
                )[16 - REACH :]

    @pl.when(has_down)
    def _():
        arrived(corner_in.at[1], halo_s.at[4], halo_r.at[4], below(side))
        for j in range(REACH):
            for tile in range(2):
                edge_f[j, tile, REACH + tile_rows : 2 * REACH + tile_rows, :] = corner_in[
                    1, j, :, tile * 128 : (tile + 1) * 128
                ].astype(jnp.float32)[:REACH]

    place = jnp.where(x == 0, tile_cols + REACH, 0)
    for j in range(REACH):
        for tile in range(2):
            for group in range(GROUPS):
                pad[pl.ds(spot_of(tile, 0, place + j, group), high, stride=GROUPS * wide), :] = edge_f[
                    j, tile, group * lines : group * lines + high, :
                ]

    def convolve(part):
        for tile in range(2):

            def body(i, _, tile=tile):
                line = part * part_rows + i // (tile_cols // 8)
                col = (i % (tile_cols // 8)) * 8
                total = jnp.broadcast_to(spread(dw_bias, tile)[None], (8, GROUPS, 128))
                for up in range(KS):
                    begin = pl.multiple_of(spot_of(tile, line + up, col, 0), 8)
                    cells = pad[pl.ds(begin, GROUPS * (7 + KS)), :].reshape(7 + KS, GROUPS, 128)
                    for j in range(KS):
                        at = ((tile * KS + up) * KS + j) * GROUPS
                        total = total + cells[j : j + 8] * taps[at : at + GROUPS, :][None]
                begin = pl.multiple_of((line * tile_cols + col) * GROUPS, 64)
                conv[tile, pl.ds(begin, 8 * GROUPS), :] = total.reshape(8 * GROUPS, 128)
                return 0

            lax.fori_loop(0, group_px // 8, body, 0)

    def cells_of(part, b):
        where = pl.ds(pl.multiple_of(part * part_regs + b * BLOCK, BLOCK), BLOCK)
        return where, [conv[tile, where, :].reshape(BLOCK // 8, 8, 128) for tile in range(2)]

    def measure(part):
        def body(b, _):
            _, cells = cells_of(part, b)
            mean = jnp.sum(cells[0] + cells[1], axis=2, keepdims=True) * (1.0 / chans)
            off = [values - mean for values in cells]
            squares = jnp.sum(off[0] * off[0] + off[1] * off[1], axis=2, keepdims=True)
            lane = lax.broadcasted_iota(jnp.int32, cells[0].shape, 2)
            turned = jnp.where(lane == 0, mean, squares).reshape(BLOCK, 128).T
            stat[part, z, pl.ds(b, 1), :] = turned[0:1]
            stat[part, z, pl.ds(STATS + b, 1), :] = turned[1:2]
            return 0

        lax.fori_loop(0, STATS, body, 0)
        for step in range(1, blks):
            send(
                lambda step=step: remote(
                    stat.at[part, z], stat.at[part, z], stat_s.at[part, step], stat_r.at[part, z],
                    at_z((z + step) % blks),
                )
            )

    def columns(index):
        return pl.ds(pl.multiple_of(index * chans, chans), chans)

    def normalize(part):
        for step in range(1, blks):
            other = (z + step) % blks
            arrived(stat.at[part, other], stat_s.at[part, step], stat_r.at[part, other], at_z(other))
        mean = sum(stat[part, o, 0:STATS] for o in range(blks)) / blks
        spread_sum = sum(
            stat[part, o, STATS : 2 * STATS] + chans * (stat[part, o, 0:STATS] - mean) ** 2 for o in range(blks)
        )
        norm_stat[0] = mean
        norm_stat[1] = lax.rsqrt(spread_sum / full + 1e-06)

        def body(b, _):
            where, cells = cells_of(part, b)
            means, scales = (
                jnp.broadcast_to(norm_stat[k, pl.ds(b, 1), :], (BLOCK, 128)).T.reshape(BLOCK // 8, 8, 128)
                for k in range(2)
            )
            for tile in range(2):
                normed = (cells[tile] - means) * scales * spread(gain, tile)[None] + spread(beta, tile)[None]
                conv[tile, where, :] = normed.reshape(BLOCK, 128)
            return 0

        lax.fori_loop(0, STATS, body, 0)
        for group in range(GROUPS):
            begin = (group % per_blk) * group_px
            for tile in range(2):
                a_send[part, group // per_blk, begin : begin + group_px, tile * 128 : (tile + 1) * 128] = conv[
                    tile, pl.ds(part * part_regs + group, group_px, stride=GROUPS), :
                ].astype(jnp.bfloat16)
        for step in range(1, blks):
            send(
                lambda step=step: remote(
                    a_send.at[part, (z + step) % blks], act.at[part, pl.ds(0, part_px), columns(z)],
                    a_s.at[part, step], a_r.at[part, z], at_z((z + step) % blks),
                )
            )
        pltpu.make_async_copy(
            a_send.at[part, z], act.at[part, pl.ds(0, part_px), columns(z)], a_l.at[part]
        ).start()
        send(
            lambda: remote(
                a_send.at[part, z], act.at[part, pl.ds(part_px, part_px), columns(z)],
                y_s.at[part, 0], y_r.at[part, z], partner,
            )
        )

    def swap_rows(part):
        for step in (1, 3, 2):
            other = (z + step) % blks
            held = act.at[part, pl.ds(0, part_px), columns(other)]
            arrived(held, a_s.at[part, step], a_r.at[part, other], at_z(other))
            send(
                lambda other=other, step=step: remote(
                    act.at[part, pl.ds(0, part_px), columns(other)],
                    act.at[part, pl.ds(part_px, part_px), columns(other)],
                    y_s.at[part, step], y_r.at[part, other], partner,
                )
            )
        pltpu.make_async_copy(
            a_send.at[part, z], act.at[part, pl.ds(0, part_px), columns(z)], a_l.at[part]
        ).wait()

    def both_ways(dist):
        return ((z >= dist, lambda: z - dist, z < blks - 1, 1), (z + dist < blks, lambda: z + dist, z > 0, -1))

    def relay(dist, k):
        block = weights[k][1]
        for cond, origin, more, step in both_ways(dist):
            spot = lambda origin=origin: block.at[origin(), pl.ds(mine, eighth)]
            when(
                cond,
                lambda spot=spot, origin=origin: arrived(spot(), zown_s.at[k, 0], z_r.at[k, origin()], side),
            )
            if dist < blks - 1:
                send(
                    lambda spot=spot, origin=origin, step=step: remote(
                        spot(), spot(), zfwd_s.at[k, origin()], z_r.at[k, origin()], at_z(z + step)
                    ),
                    cond & more,
                )
            send(
                lambda spot=spot, origin=origin: remote(
                    spot(), spot(), x_s.at[k, origin()], x_r.at[k, origin()], side
                ),
                cond,
            )
            send(
                lambda spot=spot, origin=origin: remote(
                    spot(), spot(), c_s.at[k, 0, origin()], c_r.at[k, 0, origin()], sibling
                ),
                cond,
            )

    def share(dist, k):
        block = weights[k][1]
        for cond, origin, _, _ in both_ways(dist):
            spot = lambda origin=origin: block.at[origin(), pl.ds(across, eighth)]
            when(
                cond,
                lambda spot=spot, origin=origin: arrived(
                    spot(), x_s.at[k, origin()], x_r.at[k, origin()], side
                ),
            )
            send(
                lambda spot=spot, origin=origin: remote(
                    spot(), spot(), c_s.at[k, 1, origin()], c_r.at[k, 1, origin()], sibling
                ),
                cond,
            )

    def ready():
        for copy in own:
            copy.wait()
        for step in range(1, blks):
            other = (z + step) % blks
            arrived(bias.at[other], bias_s.at[step], bias_r.at[other], at_z(other))
            for k in range(2):
                for n, column in ((0, x), (1, 1 - x)):
                    begin = pl.multiple_of(column * (half // 2) + (1 - c) * eighth, eighth)
                    arrived(
                        weights[k][1].at[other, pl.ds(begin, eighth)],
                        c_s.at[k, n, other], c_r.at[k, n, other], sibling,
                    )

    def feed(part):
        for step in range(blks):
            other = (z + step) % blks
            arrived(
                act.at[part, pl.ds(part_px, part_px), columns(other)], y_s.at[part, step], y_r.at[part, other], partner
            )

        def body(o, _):
            pre_act = lax.dot_general(
                act[part], first[o], (((1,), (1,)), ((), ())), preferred_element_type=jnp.float32
            )
            pre_act = pre_act + bias[o, 0:1, :]
            hidden = 0.5 * pre_act * (1.0 + lax.erf(pre_act * 0.7071067811865476))
            term = jnp.dot(hidden.astype(jnp.bfloat16), second[o], preferred_element_type=jnp.float32)

            @pl.when(o == 0)
            def _():
                acc[part] = term

            @pl.when(o > 0)
            def _():
                acc[part] += term

            return 0

        lax.fori_loop(0, blks, body, 0)
        for n in range(per_blk):
            rows = slice(n * group_px, (n + 1) * group_px)
            p_send[part, rows, :] = acc[part, part_px + n * group_px : part_px + (n + 1) * group_px, :].astype(
                jnp.bfloat16
            )
            send(
                lambda n=n: remote(
                    p_send.at[part, pl.ds(n * group_px, group_px)], p_in.at[part, pl.ds(n * group_px, group_px)],
                    p_s.at[part, n], p_r.at[part, n], partner,
                )
            )

    def result_rows(owner, part, n):
        begin = owner * (per_blk * lines * tile_cols) + n * (lines * tile_cols) + part * group_px
        return out.at[pl.ds(pl.multiple_of(begin, group_px), group_px)]

    def sums_for(owner, part, n):
        return r_send.at[part, pl.ds(n * group_px, group_px), columns(owner)]

    def give_back(part):
        for n in range(per_blk):
            rows = slice(n * group_px, (n + 1) * group_px)
            arrived(p_in.at[part, pl.ds(n * group_px, group_px)], p_s.at[part, n], p_r.at[part, n], partner)
            r_send[part, rows, :] = (acc[part, rows, :] + p_in[part, rows, :].astype(jnp.float32)).astype(jnp.bfloat16)
            for step in range(1, blks):
                send(
                    lambda step=step, n=n: remote(
                        sums_for((z + step) % blks, part, n), result_rows(z, part, n),
                        r_s.at[part, n, step], r_r.at[part, n, z], at_z((z + step) % blks),
                    )
                )
            pltpu.make_async_copy(sums_for(z, part, n), result_rows(z, part, n), r_l.at[part, n]).start()

    def collect(part):
        for n in range(per_blk):
            for step in range(1, blks):
                other = (z + step) % blks
                arrived(result_rows(other, part, n), r_s.at[part, n, step], r_r.at[part, n, other], at_z(other))
            pltpu.make_async_copy(sums_for(z, part, n), result_rows(z, part, n), r_l.at[part, n]).wait()

    convolve(0)
    measure(0)
    relay(1, 0)
    convolve(1)
    measure(1)
    normalize(0)
    relay(1, 1)
    share(1, 0)
    convolve(2)
    measure(2)
    normalize(1)
    relay(2, 0)
    share(1, 1)
    convolve(3)
    measure(3)
    normalize(2)
    relay(2, 1)
    normalize(3)
    share(2, 0)
    relay(3, 0)
    share(2, 1)
    relay(3, 1)
    share(3, 0)
    swap_rows(0)
    swap_rows(1)
    share(3, 1)
    swap_rows(2)
    ready()
    feed(0)
    swap_rows(3)
    feed(1)
    give_back(0)
    feed(2)
    give_back(1)
    feed(3)
    give_back(2)
    give_back(3)
    for part in range(PARTS):
        collect(part)
    for make, cond in sent:
        when(cond, lambda make=make: make().wait_send())


def fused(pixels, dw_kernel, dw_bias, ln_gain, ln_bias, w_in, b_in, w_out, b_out, layer_scale):
    tile_rows, tile_cols, chans = pixels.shape
    blks = lax.axis_size("blk")
    full = blks * chans
    hidden = w_in.shape[0]
    half = hidden // 2
    lines = tile_rows // GROUPS
    part_px = tile_rows * tile_cols // (blks * PARTS)
    pairs = GROUPS // blks
    high, wide = lines + 2 * REACH, tile_cols + 2 * REACH
    vmem, dma = pltpu.VMEM, pltpu.SemaphoreType.DMA
    anywhere = pl.BlockSpec(memory_space=pl.ANY)
    bf16, f32 = jnp.bfloat16, jnp.float32
    summed = pl.pallas_call(
        fused_kernel,
        in_specs=[pl.BlockSpec(memory_space=pltpu.HBM)] * 8,
        out_specs=anywhere,
        out_shape=jax.ShapeDtypeStruct((tile_rows * tile_cols, chans), bf16),
        scratch_shapes=[
            vmem(pixels.shape, bf16),
            vmem(dw_kernel.shape, f32),
            vmem((1, chans), f32),
            vmem((1, chans), f32),
            vmem((1, chans), f32),
            vmem((hidden // 128, 128), bf16),
            vmem((hidden // 128, 128), f32),
            dma((6,)),
            vmem((2 * high * wide * GROUPS, 128), f32),
            vmem((2 * KS * KS * GROUPS, 128), f32),
            vmem((2, lines * tile_cols * GROUPS, 128), f32),
            vmem((REACH, tile_rows, chans), bf16),
            vmem((REACH, tile_rows, chans), bf16),
            vmem((2, REACH, tile_cols, chans), bf16),
            vmem((2, REACH, 16, chans), bf16),
            vmem((REACH, 2, tile_rows + 8, 128), f32),
            vmem((PARTS, blks, 2 * STATS, 128), f32),
            vmem((2, STATS, 128), f32),
            vmem((blks, 8, half), f32),
            vmem((blks, half, full), bf16),
            vmem((blks, half, full), bf16),
            vmem((PARTS, blks, part_px, chans), bf16),
            vmem((PARTS, 2 * part_px, full), bf16),
            vmem((PARTS, 2 * part_px, full), f32),
            vmem((PARTS, part_px, full), bf16),
            vmem((PARTS, part_px, full), bf16),
            vmem((PARTS, part_px, full), bf16),
            dma((2,)), dma((5,)), dma((5,)), dma((blks,)), dma((blks,)), dma((PARTS, blks)), dma((PARTS, blks)),
            dma((2, 2)), dma((2, blks)), dma((2, blks)), dma((2, blks)), dma((2, blks)),
            dma((2, 2, blks)), dma((2, 2, blks)),
            dma((PARTS, blks)), dma((PARTS, blks)), dma((PARTS,)),
            dma((PARTS, blks)), dma((PARTS, blks)), dma((PARTS, pairs)), dma((PARTS, pairs)),
            dma((PARTS, pairs, blks)), dma((PARTS, pairs, blks)), dma((PARTS, pairs)),
        ],
        compiler_params=pltpu.CompilerParams(
            collective_id=0, has_side_effects=True, vmem_limit_bytes=64 * 1024 * 1024
        ),
    )(
        pixels, dw_kernel, dw_bias[None, :], ln_gain[None, :], ln_bias[None, :],
        b_in.reshape(hidden // 128, 128), w_in, w_out,
    )
    result = pixels.astype(f32) + layer_scale * (
        summed.astype(f32).reshape(tile_rows, tile_cols, chans) + b_out
    )
    return result.astype(bf16)


def shards(pixels, *params):
    tile_rows, tile_cols, chans = pixels.shape
    blks = lax.axis_size("blk")
    fits = (
        (lax.axis_size("y"), lax.axis_size("col"), blks, chans) == (2, 2, 4, 256)
        and (tile_rows, tile_cols) == (64, 32)
        and params[4].shape[0] % 1024 == 0
    )
    return (fused if fits else general)(pixels, *params)


def solution(mesh):
    row, col, blk = (mesh.shape[name] for name in ("row", "col", "blk"))
    split = Mesh(mesh.devices.reshape(row // 2, 2, col, blk), ("y", "core", "col", "blk"))
    placed = (
        P(("y", "core"), "col", "blk"),
        P(None, None, "blk"),
        P("blk"),
        P("blk"),
        P("blk"),
        P("blk", None),
        P("blk"),
        P("blk", None),
        P("blk"),
        P("blk"),
    )
    return jax.shard_map(
        shards, mesh=split, in_specs=placed, out_specs=P(("y", "core"), "col", "blk"), check_vma=False
    )
```

```python
import functools
import jax
import jax.numpy as jnp
from jax import lax
from jax.experimental import pallas as pl
from jax.experimental.pallas import tpu as pltpu
from jax.sharding import Mesh, PartitionSpec as P

KS = 7


def with_halo(cells, sides, width):
    for axis, dim in sides:
        count = lax.axis_size(axis)
        ends = count - 1
        head = lax.slice_in_dim(cells, 0, width, axis=dim)
        tail = lax.slice_in_dim(cells, cells.shape[dim] - width, cells.shape[dim], axis=dim)
        cells = jnp.concatenate(
            [
                lax.ppermute(tail, axis, [(i, (i + 1) % count) for i in range(ends)]),
                cells,
                lax.ppermute(head, axis, [((i + 1) % count, i) for i in range(ends)]),
            ],
            axis=dim,
        )
    return cells


def rotated(value, shift):
    count = lax.axis_size("blk")
    return lax.ppermute(value, "blk", [(i, (i + shift) % count) for i in range(count)])


def gathered(weights):
    half = weights.shape[0] // 2
    part = half // (lax.axis_size("y") * lax.axis_size("col"))
    place = lax.axis_index("y") * lax.axis_size("col") + lax.axis_index("col")
    own = lax.dynamic_slice_in_dim(
        weights, lax.axis_index("core") * half + place * part, part, axis=0
    )
    return lax.all_gather(own, ("blk", "y", "col"), axis=0, tiled=True)


def passed(w_in, b_in, w_out):
    chans = w_in.shape[1]
    half = w_in.shape[0] // 2
    plane = lax.axis_size("y") * lax.axis_size("col")
    part = half // plane
    start = lax.axis_index("core") * half
    place = lax.axis_index("y") * lax.axis_size("col") + lax.axis_index("col")
    begin = start + place * part
    bias_row = jnp.pad(
        lax.dynamic_slice_in_dim(b_in, begin, part)[None, :], ((0, 15), (0, chans - part))
    )
    own = jnp.concatenate(
        [
            lax.dynamic_slice_in_dim(w_in, begin, part, axis=0),
            lax.dynamic_slice_in_dim(w_out, begin, part, axis=0),
            bias_row,
        ]
    )
    pieces = []
    for k in range(1, lax.axis_size("blk")):
        arrived = rotated(own, k)
        pieces.append(arrived)
        for j in range(1, plane):
            pieces.append(lax.ppermute(arrived, ("y", "col"), [(i, i ^ j) for i in range(plane)]))
    w_first = [lax.dynamic_slice_in_dim(w_in, start, half, axis=0)] + [p[:part] for p in pieces]
    w_second = [lax.dynamic_slice_in_dim(w_out, start, half, axis=0)] + [
        p[part : 2 * part] for p in pieces
    ]
    bias = [lax.dynamic_slice_in_dim(b_in, start, half)] + [p[2 * part, :part] for p in pieces]
    return jnp.concatenate(w_first), jnp.concatenate(bias), jnp.concatenate(w_second)


def collected(w_in, b_in, w_out):
    half = b_in.shape[0] // 2
    b_first = lax.all_gather(
        lax.dynamic_slice_in_dim(b_in, lax.axis_index("core") * half, half),
        "blk",
        axis=0,
        tiled=True,
    )
    return gathered(w_in), b_first, gathered(w_out)


def mlp_kernel(own_ref, peer_ref, first_ref, bias_ref, second_ref, own_out, peer_out, total):
    step = pl.program_id(0)

    @pl.when(step == 0)
    def _():
        own_out[...] = jnp.zeros_like(own_out)
        total[...] = jnp.zeros_like(total)

    bias = bias_ref[...].astype(jnp.float32)
    for rows, sums in ((peer_ref, total), (own_ref, own_out)):
        pre_act = lax.dot_general(
            rows[...], first_ref[...], (((1,), (1,)), ((), ())), preferred_element_type=jnp.float32
        )
        pre_act = pre_act + bias
        hidden = 0.5 * pre_act * (1.0 + lax.erf(pre_act * 0.7071067811865476))
        sums[...] += jnp.dot(
            hidden.astype(jnp.bfloat16), second_ref[...], preferred_element_type=jnp.float32
        )

    @pl.when(step == pl.num_programs(0) - 1)
    def _():
        peer_out[...] = total[...].astype(peer_out.dtype)


def mlp_terms(own, peer, w_first, bias, w_second):
    count, chans = own.shape
    hid = w_first.shape[0]
    tile = min(1024, hid)
    whole = pl.BlockSpec((count, chans), lambda i: (0, 0))
    return pl.pallas_call(
        mlp_kernel,
        grid=(hid // tile,),
        in_specs=[
            whole,
            whole,
            pl.BlockSpec((tile, chans), lambda i: (i, 0)),
            pl.BlockSpec((1, tile), lambda i: (0, i)),
            pl.BlockSpec((tile, chans), lambda i: (i, 0)),
        ],
        out_specs=[whole, whole],
        out_shape=[
            jax.ShapeDtypeStruct((count, chans), jnp.float32),
            jax.ShapeDtypeStruct((count, chans), jnp.bfloat16),
        ],
        scratch_shapes=[pltpu.VMEM((count, chans), jnp.float32)],
        compiler_params=pltpu.CompilerParams(vmem_limit_bytes=48 * 1024 * 1024),
        cost_estimate=pl.CostEstimate(
            flops=8 * count * chans * hid, bytes_accessed=16 * count * chans, transcendentals=0
        ),
    )(own, peer, w_first, bias, w_second)


def general(pixels, dw_kernel, dw_bias, ln_gain, ln_bias, w_in, b_in, w_out, b_out, layer_scale):
    tile_rows, tile_cols, chans = pixels.shape
    reach = (KS - 1) // 2
    blks = lax.axis_size("blk")
    plane = lax.axis_size("y") * lax.axis_size("col")
    few = plane in (1, 2, 4) and blks * plane <= 32
    w_first, b_first, w_second = (passed if few else collected)(w_in, b_in, w_out)
    padded = with_halo(pixels, ((("y", "core"), 0), ("col", 1)), reach).astype(jnp.float32)
    conv_out = jnp.zeros((tile_rows, tile_cols, chans), jnp.float32) + dw_bias
    for row_off in range(KS):
        for col_off in range(KS):
            conv_out = (
                conv_out
                + padded[row_off : row_off + tile_rows, col_off : col_off + tile_cols, :]
                * dw_kernel[row_off, col_off]
            )
    part_mean = jnp.mean(conv_out, axis=-1)
    off = conv_out - part_mean[..., None]
    part_sq = jnp.sum(off * off, axis=-1)
    stats = jnp.stack([part_mean, part_sq])
    everyone = [stats] + [rotated(stats, k) for k in range(1, blks)]
    mean = sum(s[0] for s in everyone) / blks
    sq = sum(s[1] + chans * (s[0] - mean) ** 2 for s in everyone)
    spread = sq / (chans * blks)
    normed = (
        (conv_out - mean[..., None]) * lax.rsqrt(spread + 1e-06)[..., None] * ln_gain + ln_bias
    ).astype(jnp.bfloat16)
    pixel_count = tile_rows * tile_cols
    own_px = pixel_count // blks
    flat = normed.reshape(blks, own_px, chans)
    regrouped = lax.all_to_all(flat.reshape(pixel_count, chans), "blk", split_axis=0, concat_axis=1, tiled=True)
    swap = [(0, 1), (1, 0)]
    peer = lax.ppermute(regrouped, "core", swap)
    kept, sent = mlp_terms(regrouped, peer, w_first, b_first[None, :], w_second)
    mlp = kept + lax.ppermute(sent, "core", swap).astype(jnp.float32)
    mlp = mlp.astype(jnp.bfloat16)
    summed = lax.all_to_all(mlp, "blk", split_axis=1, concat_axis=0, tiled=True)
    result = pixels.astype(jnp.float32) + layer_scale * (
        summed.astype(jnp.float32).reshape(tile_rows, tile_cols, chans) + b_out
    )
    return result.astype(jnp.bfloat16)


REACH = (KS - 1) // 2
PARTS = 4
GROUPS = 8
BLOCK = 128
STATS = 4


def fused_kernel(
    px_hbm, dwk_hbm, dw_bias_hbm, gain_hbm, beta_hbm, b_in_hbm, w_in, w_out,
    out,
    px, dwk, dw_bias, gain, beta, b_in, b_all, load_sem,
    pad, taps, conv, edge, edge_in, rows_in, corner_in, edge_f, stat, norm_stat, bias,
    first, second, a_send, act, acc, p_send, p_in, r_send,
    own_sem, halo_s, halo_r, bias_s, bias_r, stat_s, stat_r,
    zown_s, zfwd_s, z_r, x_s, x_r, c_s, c_r,
    a_s, a_r, a_l, y_s, y_r, p_s, p_r, r_s, r_r, r_l,
):
    tile_rows, tile_cols, chans = px.shape
    blks = lax.axis_size("blk")
    last_row = lax.axis_size("y") * 2 - 1
    y, c, x, z = (lax.axis_index(name) for name in ("y", "core", "col", "blk"))
    row = 2 * y + c
    lines = tile_rows // GROUPS
    high, wide = lines + 2 * REACH, tile_cols + 2 * REACH
    quarter = first.shape[2]
    eighth = quarter // 2
    per_blk = GROUPS // blks
    part_rows = lines // PARTS
    group_px = part_rows * tile_cols
    part_px = per_blk * group_px
    part_regs = group_px * GROUPS
    stat_blocks = part_regs // BLOCK
    full = blks * chans

    def above(extra):
        return {"y": (row - 1) // 2, "core": (row - 1) % 2, **extra}

    def below(extra):
        return {"y": (row + 1) // 2, "core": (row + 1) % 2, **extra}

    def at_z(index):
        return {"blk": index}

    has_up, has_down = row > 0, row < last_row
    side = {"col": 1 - x}
    sibling = {"core": 1 - c}
    partner = {"y": 1 - y}

    def when(cond, act_fn):
        if cond is None:
            act_fn()
        else:
            pl.when(cond)(act_fn)

    sent = []

    def send(make, cond=None):
        when(cond, lambda: make().start())
        sent.append((make, cond))

    def remote(src, dst, send_sem, recv_sem, device):
        return pltpu.make_async_remote_copy(
            src_ref=src, dst_ref=dst, send_sem=send_sem, recv_sem=recv_sem,
            device_id=device, device_id_type=pl.DeviceIdType.MESH,
        )

    def arrived(dst, send_sem, recv_sem, device):
        remote(dst, dst, send_sem, recv_sem, device).wait_recv()

    loads = [
        pltpu.make_async_copy(src, dst, load_sem.at[k])
        for k, (src, dst) in enumerate(
            ((px_hbm, px), (dwk_hbm, dwk), (dw_bias_hbm, dw_bias), (gain_hbm, gain), (beta_hbm, beta), (b_in_hbm, b_in))
        )
    ]
    for copy in loads:
        copy.start()

    barrier = pltpu.get_barrier_semaphore()

    def greet(device):
        pl.semaphore_signal(barrier, inc=1, device_id=device, device_id_type=pl.DeviceIdType.MESH)

    for device in (side, sibling, partner):
        greet(device)
    for step in range(1, blks):
        greet(at_z((z + step) % blks))

    @pl.when(has_up)
    def _():
        greet(above({}))
        greet(above(side))

    @pl.when(has_down)
    def _():
        greet(below({}))
        greet(below(side))

    pl.semaphore_wait(barrier, 2 + blks + 2 * jnp.where(has_up, 1, 0) + 2 * jnp.where(has_down, 1, 0))

    send(lambda: remote(px_hbm.at[pl.ds(0, REACH)], rows_in.at[1], halo_s.at[0], halo_r.at[1], above({})), has_up)
    send(
        lambda: remote(
            px_hbm.at[pl.ds(tile_rows - REACH, REACH)], rows_in.at[0], halo_s.at[1], halo_r.at[0], below({})
        ),
        has_down,
    )

    quarters = (2 * y + x, 2 * y + 1 - x, 2 * (1 - y) + x)
    mine = pl.ds(pl.multiple_of(c * eighth, eighth), eighth)
    theirs = pl.ds(pl.multiple_of((1 - c) * eighth, eighth), eighth)
    start = pl.multiple_of(quarters[0] * quarter + c * eighth, eighth)
    weights = ((w_in, first), (w_out, second))

    def mate(part):
        return partner if part % 2 == 0 else side

    def own_copies(k):
        src, dst = weights[k]
        for way, cond, step in ((0, z < blks - 1, 1), (1, z > 0, -1)):
            yield cond, lambda way=way, step=step: remote(
                src.at[pl.ds(start, eighth)], dst.at[z, 0, mine],
                zown_s.at[k, way], z_r.at[k, z], at_z(z + step),
            )

    def own_out(k):
        for cond, make in own_copies(k):
            when(cond, lambda make=make: make().start())

    def own_gone(k):
        for cond, make in own_copies(k):
            when(cond, lambda make=make: make().wait_send())

    own_out(0)
    own = [
        pltpu.make_async_copy(
            src.at[pl.ds(pl.multiple_of(quarters[n] * quarter, quarter), quarter)], dst.at[z, n], own_sem.at[k, n]
        )
        for k, (src, dst) in enumerate(weights)
        for n in range(3)
    ]
    for copy in own:
        copy.start()

    def body(i, _):
        pad[pl.ds(pl.multiple_of(i * 8 * wide, 8), 8 * wide), :] = jnp.zeros((8 * wide, 128), jnp.float32)
        return 0

    lax.fori_loop(0, 2 * high, body, 0)
    for copy in loads:
        copy.wait()

    def spot_of(tile, line, col, group):
        return ((tile * high + line) * wide + col) * GROUPS + group

    def put_row(values, group, line):
        for tile in range(2):
            pad[pl.ds(spot_of(tile, line, REACH, group), tile_cols, stride=GROUPS), :] = values[
                :, tile * 128 : (tile + 1) * 128
            ]

    for group in range(GROUPS):
        low = REACH if group == 0 else 0
        top = high - (REACH if group == GROUPS - 1 else 0)

        def body(line, _, group=group):
            put_row(px[group * lines + line - REACH].astype(jnp.float32), group, line)
            return 0

        lax.fori_loop(low, top, body, 0)

    take = jnp.where(x == 0, tile_cols, REACH)
    for j in range(REACH):
        for tile in range(2):
            for group in range(GROUPS):
                edge_f[j, tile, group * lines : (group + 1) * lines, :] = pad[
                    pl.ds(spot_of(tile, REACH, take + j, group), lines, stride=GROUPS * wide), :
                ]
            edge[j, :, tile * 128 : (tile + 1) * 128] = edge_f[j, tile, 0:tile_rows, :].astype(jnp.bfloat16)
    send(lambda: remote(edge, edge_in, halo_s.at[2], halo_r.at[2], side))
    send(
        lambda: remote(edge.at[:, pl.ds(0, 16)], corner_in.at[1], halo_s.at[3], halo_r.at[4], above(side)), has_up
    )
    send(
        lambda: remote(
            edge.at[:, pl.ds(tile_rows - 16, 16)], corner_in.at[0], halo_s.at[4], halo_r.at[3], below(side)
        ),
        has_down,
    )

    b_all[z] = b_in[...].astype(jnp.float32)
    for step in range(1, blks):
        send(
            lambda step=step: remote(
                b_all.at[z], b_all.at[z], bias_s.at[step], bias_r.at[z], at_z((z + step) % blks)
            )
        )
    edge_f[...] = jnp.zeros_like(edge_f)

    def spread(ref, tile):
        return jnp.broadcast_to(ref[:, tile * 128 : (tile + 1) * 128], (GROUPS, 128))

    for tile in range(2):
        for i in range(KS):
            for j in range(KS):
                at = ((tile * KS + i) * KS + j) * GROUPS
                taps[at : at + GROUPS, :] = jnp.broadcast_to(
                    dwk[i, j : j + 1, tile * 128 : (tile + 1) * 128], (GROUPS, 128)
                )

    def finish_halo():
        @pl.when(has_up)
        def _():
            arrived(rows_in.at[0], halo_s.at[0], halo_r.at[0], above({}))
            for i in range(REACH):
                put_row(rows_in[0, i].astype(jnp.float32), 0, i)

        @pl.when(has_down)
        def _():
            arrived(rows_in.at[1], halo_s.at[1], halo_r.at[1], below({}))
            for i in range(REACH):
                put_row(rows_in[1, i].astype(jnp.float32), GROUPS - 1, high - REACH + i)

        arrived(edge_in, halo_s.at[2], halo_r.at[2], side)
        for j in range(REACH):
            for tile in range(2):
                edge_f[j, tile, REACH : REACH + tile_rows, :] = edge_in[
                    j, :, tile * 128 : (tile + 1) * 128
                ].astype(jnp.float32)

        @pl.when(has_up)
        def _():
            arrived(corner_in.at[0], halo_s.at[3], halo_r.at[3], above(side))
            for j in range(REACH):
                for tile in range(2):
                    edge_f[j, tile, 0:REACH, :] = corner_in[0, j, :, tile * 128 : (tile + 1) * 128].astype(
                        jnp.float32
                    )[16 - REACH :]

        @pl.when(has_down)
        def _():
            arrived(corner_in.at[1], halo_s.at[4], halo_r.at[4], below(side))
            for j in range(REACH):
                for tile in range(2):
                    edge_f[j, tile, REACH + tile_rows : 2 * REACH + tile_rows, :] = corner_in[
                        1, j, :, tile * 128 : (tile + 1) * 128
                    ].astype(jnp.float32)[:REACH]

        place = jnp.where(x == 0, tile_cols + REACH, 0)
        for j in range(REACH):
            for tile in range(2):
                for group in range(GROUPS):
                    pad[pl.ds(spot_of(tile, 0, place + j, group), high, stride=GROUPS * wide), :] = edge_f[
                        j, tile, group * lines : group * lines + high, :
                    ]

    def convolve(part):
        for tile in range(2):

            def body(i, _, tile=tile):
                line = part * part_rows + i // (tile_cols // 8)
                col = (i % (tile_cols // 8)) * 8
                total = jnp.broadcast_to(spread(dw_bias, tile)[None], (8, GROUPS, 128))
                for up in range(KS):
                    begin = pl.multiple_of(spot_of(tile, line + up, col, 0), 8)
                    cells = pad[pl.ds(begin, GROUPS * (7 + KS)), :].reshape(7 + KS, GROUPS, 128)
                    for j in range(KS):
                        at = ((tile * KS + up) * KS + j) * GROUPS
                        total = total + cells[j : j + 8] * taps[at : at + GROUPS, :][None]
                begin = pl.multiple_of((line * tile_cols + col) * GROUPS, 64)
                conv[tile, pl.ds(begin, 8 * GROUPS), :] = total.reshape(8 * GROUPS, 128)
                return 0

            lax.fori_loop(0, group_px // 8, body, 0)

    def cells_of(part, b):
        where = pl.ds(pl.multiple_of(part * part_regs + b * BLOCK, BLOCK), BLOCK)
        return where, [conv[tile, where, :].reshape(BLOCK // 8, 8, 128) for tile in range(2)]

    def measure(part):
        def body(b, _):
            _, cells = cells_of(part, b)
            mean = jnp.sum(cells[0] + cells[1], axis=2, keepdims=True) * (1.0 / chans)
            off = [values - mean for values in cells]
            squares = jnp.sum(off[0] * off[0] + off[1] * off[1], axis=2, keepdims=True)
            lane = lax.broadcasted_iota(jnp.int32, cells[0].shape, 2)
            turned = jnp.where(lane == 0, mean, squares).reshape(BLOCK, 128).T
            stat[part, z, pl.ds(b, 1), :] = turned[0:1]
            stat[part, z, pl.ds(STATS + b, 1), :] = turned[1:2]
            return 0

        lax.fori_loop(0, STATS, body, 0)
        for step in range(1, blks):
            send(
                lambda step=step: remote(
                    stat.at[part, z], stat.at[part, z], stat_s.at[part, step], stat_r.at[part, z],
                    at_z((z + step) % blks),
                )
            )

    def columns(index):
        return pl.ds(pl.multiple_of(index * chans, chans), chans)

    def normalize(part):
        for step in range(1, blks):
            other = (z + step) % blks
            arrived(stat.at[part, other], stat_s.at[part, step], stat_r.at[part, other], at_z(other))
        mean = sum(stat[part, o, 0:STATS] for o in range(blks)) / blks
        spread_sum = sum(
            stat[part, o, STATS : 2 * STATS] + chans * (stat[part, o, 0:STATS] - mean) ** 2 for o in range(blks)
        )
        norm_stat[0] = mean
        norm_stat[1] = lax.rsqrt(spread_sum / full + 1e-06)

        def body(b, _):
            where, cells = cells_of(part, b)
            means, scales = (
                jnp.broadcast_to(norm_stat[k, pl.ds(b, 1), :], (BLOCK, 128)).T.reshape(BLOCK // 8, 8, 128)
                for k in range(2)
            )
            for tile in range(2):
                normed = (cells[tile] - means) * scales * spread(gain, tile)[None] + spread(beta, tile)[None]
                conv[tile, where, :] = normed.reshape(BLOCK, 128)
            return 0

        lax.fori_loop(0, STATS, body, 0)
        for group in range(GROUPS):
            begin = (group % per_blk) * group_px
            for tile in range(2):
                a_send[part, group // per_blk, begin : begin + group_px, tile * 128 : (tile + 1) * 128] = conv[
                    tile, pl.ds(part * part_regs + group, group_px, stride=GROUPS), :
                ].astype(jnp.bfloat16)
        pltpu.make_async_copy(
            a_send.at[part, z], act.at[part, pl.ds(0, part_px), columns(z)], a_l.at[part]
        ).start()
        send(
            lambda: remote(
                a_send.at[part, z], act.at[part, pl.ds(part_px, part_px), columns(z)],
                y_s.at[part, 0], y_r.at[part, z], mate(part),
            )
        )

    def regroup(part):
        for step in (2, 1, 3):
            send(
                lambda step=step: remote(
                    a_send.at[part, (z + step) % blks], act.at[part, pl.ds(0, part_px), columns(z)],
                    a_s.at[part, step], a_r.at[part, z], at_z((z + step) % blks),
                )
            )

    def swap_rows(part):
        for step in (1, 3, 2):
            other = (z + step) % blks
            held = act.at[part, pl.ds(0, part_px), columns(other)]
            arrived(held, a_s.at[part, step], a_r.at[part, other], at_z(other))
            send(
                lambda other=other, step=step: remote(
                    act.at[part, pl.ds(0, part_px), columns(other)],
                    act.at[part, pl.ds(part_px, part_px), columns(other)],
                    y_s.at[part, step], y_r.at[part, other], mate(part),
                )
            )
        pltpu.make_async_copy(
            a_send.at[part, z], act.at[part, pl.ds(0, part_px), columns(z)], a_l.at[part]
        ).wait()

    def both_ways(dist):
        return ((z >= dist, lambda: z - dist, z < blks - 1, 1), (z + dist < blks, lambda: z + dist, z > 0, -1))

    def passed_on(dist, k):
        block = weights[k][1]
        for cond, origin, more, step in both_ways(dist):
            spot = lambda origin=origin: block.at[origin(), 0, mine]
            yield cond & more, lambda spot=spot, origin=origin, step=step: remote(
                spot(), spot(), zfwd_s.at[k, origin()], z_r.at[k, origin()], at_z(z + step)
            )

    def forward(dist, k):
        for cond, make in passed_on(dist, k):
            when(cond, lambda make=make: make().start())

    def forwarded(dist, k):
        for cond, make in passed_on(dist, k):
            when(cond, lambda make=make: make().wait_send())

    def take_in(dist, k):
        block = weights[k][1]
        for cond, origin, _, _ in both_ways(dist):
            spot = lambda origin=origin: block.at[origin(), 0, mine]
            when(
                cond,
                lambda spot=spot, origin=origin: arrived(spot(), zown_s.at[k, 0], z_r.at[k, origin()], side),
            )
            for n, device in ((1, side), (2, partner)):
                send(
                    lambda spot=spot, origin=origin, n=n, device=device: remote(
                        spot(), block.at[origin(), n, mine], x_s.at[k, n - 1, origin()], x_r.at[k, n - 1, origin()],
                        device,
                    ),
                    cond,
                )
            send(
                lambda spot=spot, origin=origin: remote(
                    spot(), spot(), c_s.at[k, 0, origin()], c_r.at[k, 0, origin()], sibling
                ),
                cond,
            )

    def share(dist, k):
        block = weights[k][1]
        for cond, origin, _, _ in both_ways(dist):
            for n, device in ((1, side), (2, partner)):
                spot = lambda origin=origin, n=n: block.at[origin(), n, mine]
                when(
                    cond,
                    lambda spot=spot, origin=origin, n=n, device=device: arrived(
                        spot(), x_s.at[k, n - 1, origin()], x_r.at[k, n - 1, origin()], device
                    ),
                )
                send(
                    lambda spot=spot, origin=origin, n=n: remote(
                        spot(), spot(), c_s.at[k, n, origin()], c_r.at[k, n, origin()], sibling
                    ),
                    cond,
                )

    def ready():
        for copy in own:
            copy.wait()
        for step in range(1, blks):
            other = (z + step) % blks
            arrived(b_all.at[other], bias_s.at[step], bias_r.at[other], at_z(other))
            for k in range(2):
                for n in range(3):
                    arrived(weights[k][1].at[other, n, theirs], c_s.at[k, n, other], c_r.at[k, n, other], sibling)
        wide_rows = quarter // 128
        for o in range(blks):
            for n in range(3):
                for k in range(wide_rows):
                    bias[o, n, :, k * 128 : (k + 1) * 128] = jnp.broadcast_to(
                        b_all[o, pl.ds(quarters[n] * wide_rows + k, 1), :], (8, 128)
                    )

    def feed(part):
        for step in range(blks):
            other = (z + step) % blks
            arrived(
                act.at[part, pl.ds(part_px, part_px), columns(other)], y_s.at[part, step], y_r.at[part, other], mate(part)
            )

        def hidden_of(o, n):
            pre_act = lax.dot_general(
                act[part], first[o, n], (((1,), (1,)), ((), ())), preferred_element_type=jnp.float32
            )
            pre_act = pre_act + bias[o, n, 0:1, :]
            return (0.5 * pre_act * (1.0 + lax.erf(pre_act * 0.7071067811865476))).astype(jnp.bfloat16)

        def body(o, _):
            term = sum(
                jnp.dot(hidden_of(o, n), second[o, n], preferred_element_type=jnp.float32)
                for n in (0, 1 + part % 2)
            )

            @pl.when(o == 0)
            def _():
                acc[part] = term

            @pl.when(o > 0)
            def _():
                acc[part] += term

            return 0

        lax.fori_loop(0, blks, body, 0)
        for n in range(per_blk):
            rows = slice(n * group_px, (n + 1) * group_px)
            p_send[part, rows, :] = acc[part, part_px + n * group_px : part_px + (n + 1) * group_px, :].astype(
                jnp.bfloat16
            )
            send(
                lambda n=n: remote(
                    p_send.at[part, pl.ds(n * group_px, group_px)], p_in.at[part, pl.ds(n * group_px, group_px)],
                    p_s.at[part, n], p_r.at[part, n], mate(part),
                )
            )

    def result_rows(owner, part, n):
        begin = owner * (per_blk * lines * tile_cols) + n * (lines * tile_cols) + part * group_px
        return out.at[pl.ds(pl.multiple_of(begin, group_px), group_px)]

    def sums_for(owner, part, n):
        return r_send.at[part, pl.ds(n * group_px, group_px), columns(owner)]

    def give_back(part):
        for n in range(per_blk):
            rows = slice(n * group_px, (n + 1) * group_px)
            arrived(p_in.at[part, pl.ds(n * group_px, group_px)], p_s.at[part, n], p_r.at[part, n], mate(part))
            r_send[part, rows, :] = (acc[part, rows, :] + p_in[part, rows, :].astype(jnp.float32)).astype(jnp.bfloat16)
            for step in range(1, blks):
                send(
                    lambda step=step, n=n: remote(
                        sums_for((z + step) % blks, part, n), result_rows(z, part, n),
                        r_s.at[part, n, step], r_r.at[part, n, z], at_z((z + step) % blks),
                    )
                )
            pltpu.make_async_copy(sums_for(z, part, n), result_rows(z, part, n), r_l.at[part, n]).start()

    def collect(part):
        for n in range(per_blk):
            for step in range(1, blks):
                other = (z + step) % blks
                arrived(result_rows(other, part, n), r_s.at[part, n, step], r_r.at[part, n, other], at_z(other))
            pltpu.make_async_copy(sums_for(z, part, n), result_rows(z, part, n), r_l.at[part, n]).wait()

    own_gone(0)
    own_out(1)
    take_in(1, 0)
    finish_halo()
    convolve(0)
    measure(0)
    own_gone(1)
    forward(1, 0)
    take_in(1, 1)
    convolve(1)
    measure(1)
    normalize(0)
    forwarded(1, 0)
    forward(1, 1)
    take_in(2, 0)
    share(1, 0)
    convolve(2)
    measure(2)
    normalize(1)
    forwarded(1, 1)
    forward(2, 0)
    take_in(2, 1)
    regroup(0)
    share(1, 1)
    convolve(3)
    measure(3)
    normalize(2)
    forwarded(2, 0)
    forward(2, 1)
    take_in(3, 0)
    share(2, 0)
    normalize(3)
    swap_rows(0)
    regroup(1)
    forwarded(2, 1)
    take_in(3, 1)
    share(2, 1)
    share(3, 0)
    swap_rows(1)
    regroup(2)
    share(3, 1)
    swap_rows(2)
    regroup(3)
    ready()
    feed(0)
    swap_rows(3)
    feed(1)
    give_back(0)
    feed(2)
    give_back(1)
    feed(3)
    give_back(2)
    give_back(3)
    for part in range(PARTS):
        collect(part)
    for make, cond in sent:
        when(cond, lambda make=make: make().wait_send())


def fused(pixels, dw_kernel, dw_bias, ln_gain, ln_bias, w_in, b_in, w_out, b_out, layer_scale):
    tile_rows, tile_cols, chans = pixels.shape
    blks = lax.axis_size("blk")
    full = blks * chans
    hidden = w_in.shape[0]
    lines = tile_rows // GROUPS
    part_px = tile_rows * tile_cols // (blks * PARTS)
    pairs = GROUPS // blks
    high, wide = lines + 2 * REACH, tile_cols + 2 * REACH
    vmem, dma = pltpu.VMEM, pltpu.SemaphoreType.DMA
    anywhere = pl.BlockSpec(memory_space=pl.ANY)
    bf16, f32 = jnp.bfloat16, jnp.float32
    summed = pl.pallas_call(
        fused_kernel,
        in_specs=[pl.BlockSpec(memory_space=pltpu.HBM)] * 8,
        out_specs=anywhere,
        out_shape=jax.ShapeDtypeStruct((tile_rows * tile_cols, chans), bf16),
        scratch_shapes=[
            vmem(pixels.shape, bf16),
            vmem(dw_kernel.shape, f32),
            vmem((1, chans), f32),
            vmem((1, chans), f32),
            vmem((1, chans), f32),
            vmem((hidden // 128, 128), bf16),
            vmem((blks, hidden // 128, 128), f32),
            dma((6,)),
            vmem((2 * high * wide * GROUPS, 128), f32),
            vmem((2 * KS * KS * GROUPS, 128), f32),
            vmem((2, lines * tile_cols * GROUPS, 128), f32),
            vmem((REACH, tile_rows, chans), bf16),
            vmem((REACH, tile_rows, chans), bf16),
            vmem((2, REACH, tile_cols, chans), bf16),
            vmem((2, REACH, 16, chans), bf16),
            vmem((REACH, 2, tile_rows + 8, 128), f32),
            vmem((PARTS, blks, 2 * STATS, 128), f32),
            vmem((2, STATS, 128), f32),
            vmem((blks, 3, 8, hidden // 4), f32),
            vmem((blks, 3, hidden // 4, full), bf16),
            vmem((blks, 3, hidden // 4, full), bf16),
            vmem((PARTS, blks, part_px, chans), bf16),
            vmem((PARTS, 2 * part_px, full), bf16),
            vmem((PARTS, 2 * part_px, full), f32),
            vmem((PARTS, part_px, full), bf16),
            vmem((PARTS, part_px, full), bf16),
            vmem((PARTS, part_px, full), bf16),
            dma((2, 3)), dma((5,)), dma((5,)), dma((blks,)), dma((blks,)), dma((PARTS, blks)), dma((PARTS, blks)),
            dma((2, 2)), dma((2, blks)), dma((2, blks)), dma((2, 2, blks)), dma((2, 2, blks)),
            dma((2, 3, blks)), dma((2, 3, blks)),
            dma((PARTS, blks)), dma((PARTS, blks)), dma((PARTS,)),
            dma((PARTS, blks)), dma((PARTS, blks)), dma((PARTS, pairs)), dma((PARTS, pairs)),
            dma((PARTS, pairs, blks)), dma((PARTS, pairs, blks)), dma((PARTS, pairs)),
        ],
        compiler_params=pltpu.CompilerParams(
            collective_id=0, has_side_effects=True, vmem_limit_bytes=64 * 1024 * 1024
        ),
    )(
        pixels, dw_kernel, dw_bias[None, :], ln_gain[None, :], ln_bias[None, :],
        b_in.reshape(hidden // 128, 128), w_in, w_out,
    )
    result = pixels.astype(f32) + layer_scale * (
        summed.astype(f32).reshape(tile_rows, tile_cols, chans) + b_out
    )
    return result.astype(bf16)


def shards(pixels, *params):
    tile_rows, tile_cols, chans = pixels.shape
    blks = lax.axis_size("blk")
    fits = (
        (lax.axis_size("y"), lax.axis_size("col"), blks, chans) == (2, 2, 4, 256)
        and (tile_rows, tile_cols) == (64, 32)
        and params[4].shape[0] % 1024 == 0
    )
    return (fused if fits else general)(pixels, *params)


def solution(mesh):
    row, col, blk = (mesh.shape[name] for name in ("row", "col", "blk"))
    split = Mesh(mesh.devices.reshape(row // 2, 2, col, blk), ("y", "core", "col", "blk"))
    placed = (
        P(("y", "core"), "col", "blk"),
        P(None, None, "blk"),
        P("blk"),
        P("blk"),
        P("blk"),
        P("blk", None),
        P("blk"),
        P("blk", None),
        P("blk"),
        P("blk"),
    )
    return jax.shard_map(
        shards, mesh=split, in_specs=placed, out_specs=P(("y", "core"), "col", "blk"), check_vma=False
    )
```

```python
import functools
import jax
import jax.numpy as jnp
from jax import lax
from jax.experimental import pallas as pl
from jax.experimental.pallas import tpu as pltpu
from jax.sharding import Mesh, PartitionSpec as P

KS = 7


def with_halo(cells, sides, width):
    for axis, dim in sides:
        count = lax.axis_size(axis)
        ends = count - 1
        head = lax.slice_in_dim(cells, 0, width, axis=dim)
        tail = lax.slice_in_dim(cells, cells.shape[dim] - width, cells.shape[dim], axis=dim)
        cells = jnp.concatenate(
            [
                lax.ppermute(tail, axis, [(i, (i + 1) % count) for i in range(ends)]),
                cells,
                lax.ppermute(head, axis, [((i + 1) % count, i) for i in range(ends)]),
            ],
            axis=dim,
        )
    return cells


def rotated(value, shift):
    count = lax.axis_size("blk")
    return lax.ppermute(value, "blk", [(i, (i + shift) % count) for i in range(count)])


def gathered(weights):
    half = weights.shape[0] // 2
    part = half // (lax.axis_size("y") * lax.axis_size("col"))
    place = lax.axis_index("y") * lax.axis_size("col") + lax.axis_index("col")
    own = lax.dynamic_slice_in_dim(
        weights, lax.axis_index("core") * half + place * part, part, axis=0
    )
    return lax.all_gather(own, ("blk", "y", "col"), axis=0, tiled=True)


def passed(w_in, b_in, w_out):
    chans = w_in.shape[1]
    half = w_in.shape[0] // 2
    plane = lax.axis_size("y") * lax.axis_size("col")
    part = half // plane
    start = lax.axis_index("core") * half
    place = lax.axis_index("y") * lax.axis_size("col") + lax.axis_index("col")
    begin = start + place * part
    bias_row = jnp.pad(
        lax.dynamic_slice_in_dim(b_in, begin, part)[None, :], ((0, 15), (0, chans - part))
    )
    own = jnp.concatenate(
        [
            lax.dynamic_slice_in_dim(w_in, begin, part, axis=0),
            lax.dynamic_slice_in_dim(w_out, begin, part, axis=0),
            bias_row,
        ]
    )
    pieces = []
    for k in range(1, lax.axis_size("blk")):
        arrived = rotated(own, k)
        pieces.append(arrived)
        for j in range(1, plane):
            pieces.append(lax.ppermute(arrived, ("y", "col"), [(i, i ^ j) for i in range(plane)]))
    w_first = [lax.dynamic_slice_in_dim(w_in, start, half, axis=0)] + [p[:part] for p in pieces]
    w_second = [lax.dynamic_slice_in_dim(w_out, start, half, axis=0)] + [
        p[part : 2 * part] for p in pieces
    ]
    bias = [lax.dynamic_slice_in_dim(b_in, start, half)] + [p[2 * part, :part] for p in pieces]
    return jnp.concatenate(w_first), jnp.concatenate(bias), jnp.concatenate(w_second)


def collected(w_in, b_in, w_out):
    half = b_in.shape[0] // 2
    b_first = lax.all_gather(
        lax.dynamic_slice_in_dim(b_in, lax.axis_index("core") * half, half),
        "blk",
        axis=0,
        tiled=True,
    )
    return gathered(w_in), b_first, gathered(w_out)


def mlp_kernel(own_ref, peer_ref, first_ref, bias_ref, second_ref, own_out, peer_out, total):
    step = pl.program_id(0)

    @pl.when(step == 0)
    def _():
        own_out[...] = jnp.zeros_like(own_out)
        total[...] = jnp.zeros_like(total)

    bias = bias_ref[...].astype(jnp.float32)
    for rows, sums in ((peer_ref, total), (own_ref, own_out)):
        pre_act = lax.dot_general(
            rows[...], first_ref[...], (((1,), (1,)), ((), ())), preferred_element_type=jnp.float32
        )
        pre_act = pre_act + bias
        hidden = 0.5 * pre_act * (1.0 + lax.erf(pre_act * 0.7071067811865476))
        sums[...] += jnp.dot(
            hidden.astype(jnp.bfloat16), second_ref[...], preferred_element_type=jnp.float32
        )

    @pl.when(step == pl.num_programs(0) - 1)
    def _():
        peer_out[...] = total[...].astype(peer_out.dtype)


def mlp_terms(own, peer, w_first, bias, w_second):
    count, chans = own.shape
    hid = w_first.shape[0]
    tile = min(1024, hid)
    whole = pl.BlockSpec((count, chans), lambda i: (0, 0))
    return pl.pallas_call(
        mlp_kernel,
        grid=(hid // tile,),
        in_specs=[
            whole,
            whole,
            pl.BlockSpec((tile, chans), lambda i: (i, 0)),
            pl.BlockSpec((1, tile), lambda i: (0, i)),
            pl.BlockSpec((tile, chans), lambda i: (i, 0)),
        ],
        out_specs=[whole, whole],
        out_shape=[
            jax.ShapeDtypeStruct((count, chans), jnp.float32),
            jax.ShapeDtypeStruct((count, chans), jnp.bfloat16),
        ],
        scratch_shapes=[pltpu.VMEM((count, chans), jnp.float32)],
        compiler_params=pltpu.CompilerParams(vmem_limit_bytes=48 * 1024 * 1024),
        cost_estimate=pl.CostEstimate(
            flops=8 * count * chans * hid, bytes_accessed=16 * count * chans, transcendentals=0
        ),
    )(own, peer, w_first, bias, w_second)


def general(pixels, dw_kernel, dw_bias, ln_gain, ln_bias, w_in, b_in, w_out, b_out, layer_scale):
    tile_rows, tile_cols, chans = pixels.shape
    reach = (KS - 1) // 2
    blks = lax.axis_size("blk")
    plane = lax.axis_size("y") * lax.axis_size("col")
    few = plane in (1, 2, 4) and blks * plane <= 32
    w_first, b_first, w_second = (passed if few else collected)(w_in, b_in, w_out)
    padded = with_halo(pixels, ((("y", "core"), 0), ("col", 1)), reach).astype(jnp.float32)
    conv_out = jnp.zeros((tile_rows, tile_cols, chans), jnp.float32) + dw_bias
    for row_off in range(KS):
        for col_off in range(KS):
            conv_out = (
                conv_out
                + padded[row_off : row_off + tile_rows, col_off : col_off + tile_cols, :]
                * dw_kernel[row_off, col_off]
            )
    part_mean = jnp.mean(conv_out, axis=-1)
    off = conv_out - part_mean[..., None]
    part_sq = jnp.sum(off * off, axis=-1)
    stats = jnp.stack([part_mean, part_sq])
    everyone = [stats] + [rotated(stats, k) for k in range(1, blks)]
    mean = sum(s[0] for s in everyone) / blks
    sq = sum(s[1] + chans * (s[0] - mean) ** 2 for s in everyone)
    spread = sq / (chans * blks)
    normed = (
        (conv_out - mean[..., None]) * lax.rsqrt(spread + 1e-06)[..., None] * ln_gain + ln_bias
    ).astype(jnp.bfloat16)
    pixel_count = tile_rows * tile_cols
    own_px = pixel_count // blks
    flat = normed.reshape(blks, own_px, chans)
    regrouped = lax.all_to_all(flat.reshape(pixel_count, chans), "blk", split_axis=0, concat_axis=1, tiled=True)
    swap = [(0, 1), (1, 0)]
    peer = lax.ppermute(regrouped, "core", swap)
    kept, sent = mlp_terms(regrouped, peer, w_first, b_first[None, :], w_second)
    mlp = kept + lax.ppermute(sent, "core", swap).astype(jnp.float32)
    mlp = mlp.astype(jnp.bfloat16)
    summed = lax.all_to_all(mlp, "blk", split_axis=1, concat_axis=0, tiled=True)
    result = pixels.astype(jnp.float32) + layer_scale * (
        summed.astype(jnp.float32).reshape(tile_rows, tile_cols, chans) + b_out
    )
    return result.astype(jnp.bfloat16)


REACH = (KS - 1) // 2
PARTS = 4
GROUPS = 8
CUTS = 2
BLOCK = 128
STATS = 4


def fused_kernel(
    px_hbm, dwk_hbm, dw_bias_hbm, gain_hbm, beta_hbm, b_in_hbm, w_in, w_out,
    out,
    px, dwk, dw_bias, gain, beta, b_in, b_all, load_sem,
    pad, taps, conv, edge, edge_in, rows_in, corner_in, edge_f, stat, norm_stat, bias,
    first, second, a_send, act, acc, p_send, p_in, r_send,
    own_sem, halo_s, halo_r, bias_s, bias_r, stat_s, stat_r,
    zown_s, zfwd_s, z_r, x_s, x_r, c_s, c_r,
    a_s, a_r, a_l, y_s, y_r, p_s, p_r, r_s, r_r, r_l,
):
    tile_rows, tile_cols, chans = px.shape
    blks = lax.axis_size("blk")
    last_row = lax.axis_size("y") * 2 - 1
    y, c, x, z = (lax.axis_index(name) for name in ("y", "core", "col", "blk"))
    row = 2 * y + c
    lines = tile_rows // GROUPS
    high, wide = lines + 2 * REACH, tile_cols + 2 * REACH
    quarter = first.shape[2]
    eighth = quarter // 2
    per_blk = GROUPS // blks
    part_rows = lines // PARTS
    group_px = part_rows * tile_cols
    part_px = per_blk * group_px
    part_regs = group_px * GROUPS
    stat_blocks = part_regs // BLOCK
    full = blks * chans

    def above(extra):
        return {"y": (row - 1) // 2, "core": (row - 1) % 2, **extra}

    def below(extra):
        return {"y": (row + 1) // 2, "core": (row + 1) % 2, **extra}

    def at_z(index):
        return {"blk": index}

    has_up, has_down = row > 0, row < last_row
    side = {"col": 1 - x}
    sibling = {"core": 1 - c}
    partner = {"y": 1 - y}

    def when(cond, act_fn):
        if cond is None:
            act_fn()
        else:
            pl.when(cond)(act_fn)

    sent = []

    def send(make, cond=None):
        when(cond, lambda: make().start())
        sent.append((make, cond))

    def remote(src, dst, send_sem, recv_sem, device):
        return pltpu.make_async_remote_copy(
            src_ref=src, dst_ref=dst, send_sem=send_sem, recv_sem=recv_sem,
            device_id=device, device_id_type=pl.DeviceIdType.MESH,
        )

    def arrived(dst, send_sem, recv_sem, device):
        remote(dst, dst, send_sem, recv_sem, device).wait_recv()

    loads = [
        pltpu.make_async_copy(src, dst, load_sem.at[k])
        for k, (src, dst) in enumerate(
            ((px_hbm, px), (dwk_hbm, dwk), (dw_bias_hbm, dw_bias), (gain_hbm, gain), (beta_hbm, beta), (b_in_hbm, b_in))
        )
    ]
    for copy in loads:
        copy.start()

    barrier = pltpu.get_barrier_semaphore()

    def greet(device):
        pl.semaphore_signal(barrier, inc=1, device_id=device, device_id_type=pl.DeviceIdType.MESH)

    for device in (side, sibling, partner):
        greet(device)
    for step in range(1, blks):
        greet(at_z((z + step) % blks))

    @pl.when(has_up)
    def _():
        greet(above({}))
        greet(above(side))

    @pl.when(has_down)
    def _():
        greet(below({}))
        greet(below(side))

    pl.semaphore_wait(barrier, 2 + blks + 2 * jnp.where(has_up, 1, 0) + 2 * jnp.where(has_down, 1, 0))

    send(lambda: remote(px_hbm.at[pl.ds(0, REACH)], rows_in.at[1], halo_s.at[0], halo_r.at[1], above({})), has_up)
    send(
        lambda: remote(
            px_hbm.at[pl.ds(tile_rows - REACH, REACH)], rows_in.at[0], halo_s.at[1], halo_r.at[0], below({})
        ),
        has_down,
    )

    quarters = (2 * y + x, 2 * y + 1 - x, 2 * (1 - y) + x)
    start = pl.multiple_of(quarters[0] * quarter + c * eighth, eighth)
    weights = tuple((src, dst, n) for src, dst in ((w_in, first), (w_out, second)) for n in range(CUTS))
    cut = eighth // CUTS

    def spot_for(k, origin, n, core):
        begin = pl.multiple_of(core * eighth + weights[k][2] * cut, cut)
        return weights[k][1].at[origin, n, pl.ds(begin, cut)]

    def each(k):
        return range(k * CUTS, (k + 1) * CUTS)


    def mate(part):
        return partner if part % 2 == 0 else side

    def own_copies(k):
        src, _, n = weights[k]
        for way, cond, step in ((0, z < blks - 1, 1), (1, z > 0, -1)):
            yield cond, lambda way=way, step=step: remote(
                src.at[pl.ds(pl.multiple_of(start + n * cut, cut), cut)], spot_for(k, z, 0, c),
                zown_s.at[k, way], z_r.at[k, z], at_z(z + step),
            )

    def own_out(k):
        for cond, make in (pair for j in each(k) for pair in own_copies(j)):
            when(cond, lambda make=make: make().start())

    def own_gone(k):
        for cond, make in (pair for j in each(k) for pair in own_copies(j)):
            when(cond, lambda make=make: make().wait_send())

    own_out(0)
    own = [
        pltpu.make_async_copy(
            src.at[pl.ds(pl.multiple_of(quarters[n] * quarter, quarter), quarter)], dst.at[z, n], own_sem.at[k, n]
        )
        for k, (src, dst) in enumerate(((w_in, first), (w_out, second)))
        for n in range(3)
    ]
    for copy in own:
        copy.start()

    def body(i, _):
        pad[pl.ds(pl.multiple_of(i * 8 * wide, 8), 8 * wide), :] = jnp.zeros((8 * wide, 128), jnp.float32)
        return 0

    lax.fori_loop(0, 2 * high, body, 0)
    for copy in loads:
        copy.wait()

    def spot_of(tile, line, col, group):
        return ((tile * high + line) * wide + col) * GROUPS + group

    def put_row(values, group, line):
        for tile in range(2):
            pad[pl.ds(spot_of(tile, line, REACH, group), tile_cols, stride=GROUPS), :] = values[
                :, tile * 128 : (tile + 1) * 128
            ]

    for group in range(GROUPS):
        low = REACH if group == 0 else 0
        top = high - (REACH if group == GROUPS - 1 else 0)

        def body(line, _, group=group):
            put_row(px[group * lines + line - REACH].astype(jnp.float32), group, line)
            return 0

        lax.fori_loop(low, top, body, 0)

    take = jnp.where(x == 0, tile_cols, REACH)
    for j in range(REACH):
        for tile in range(2):
            for group in range(GROUPS):
                edge_f[j, tile, group * lines : (group + 1) * lines, :] = pad[
                    pl.ds(spot_of(tile, REACH, take + j, group), lines, stride=GROUPS * wide), :
                ]
            edge[j, :, tile * 128 : (tile + 1) * 128] = edge_f[j, tile, 0:tile_rows, :].astype(jnp.bfloat16)
    send(lambda: remote(edge, edge_in, halo_s.at[2], halo_r.at[2], side))
    send(
        lambda: remote(edge.at[:, pl.ds(0, 16)], corner_in.at[1], halo_s.at[3], halo_r.at[4], above(side)), has_up
    )
    send(
        lambda: remote(
            edge.at[:, pl.ds(tile_rows - 16, 16)], corner_in.at[0], halo_s.at[4], halo_r.at[3], below(side)
        ),
        has_down,
    )

    b_all[z] = b_in[...].astype(jnp.float32)
    for step in range(1, blks):
        send(
            lambda step=step: remote(
                b_all.at[z], b_all.at[z], bias_s.at[step], bias_r.at[z], at_z((z + step) % blks)
            )
        )
    edge_f[...] = jnp.zeros_like(edge_f)

    def spread(ref, tile):
        return jnp.broadcast_to(ref[:, tile * 128 : (tile + 1) * 128], (GROUPS, 128))

    for tile in range(2):
        for i in range(KS):
            for j in range(KS):
                at = ((tile * KS + i) * KS + j) * GROUPS
                taps[at : at + GROUPS, :] = jnp.broadcast_to(
                    dwk[i, j : j + 1, tile * 128 : (tile + 1) * 128], (GROUPS, 128)
                )

    def finish_halo():
        @pl.when(has_up)
        def _():
            arrived(rows_in.at[0], halo_s.at[0], halo_r.at[0], above({}))
            for i in range(REACH):
                put_row(rows_in[0, i].astype(jnp.float32), 0, i)

        @pl.when(has_down)
        def _():
            arrived(rows_in.at[1], halo_s.at[1], halo_r.at[1], below({}))
            for i in range(REACH):
                put_row(rows_in[1, i].astype(jnp.float32), GROUPS - 1, high - REACH + i)

        arrived(edge_in, halo_s.at[2], halo_r.at[2], side)
        for j in range(REACH):
            for tile in range(2):
                edge_f[j, tile, REACH : REACH + tile_rows, :] = edge_in[
                    j, :, tile * 128 : (tile + 1) * 128
                ].astype(jnp.float32)

        @pl.when(has_up)
        def _():
            arrived(corner_in.at[0], halo_s.at[3], halo_r.at[3], above(side))
            for j in range(REACH):
                for tile in range(2):
                    edge_f[j, tile, 0:REACH, :] = corner_in[0, j, :, tile * 128 : (tile + 1) * 128].astype(
                        jnp.float32
                    )[16 - REACH :]

        @pl.when(has_down)
        def _():
            arrived(corner_in.at[1], halo_s.at[4], halo_r.at[4], below(side))
            for j in range(REACH):
                for tile in range(2):
                    edge_f[j, tile, REACH + tile_rows : 2 * REACH + tile_rows, :] = corner_in[
                        1, j, :, tile * 128 : (tile + 1) * 128
                    ].astype(jnp.float32)[:REACH]

        place = jnp.where(x == 0, tile_cols + REACH, 0)
        for j in range(REACH):
            for tile in range(2):
                for group in range(GROUPS):
                    pad[pl.ds(spot_of(tile, 0, place + j, group), high, stride=GROUPS * wide), :] = edge_f[
                        j, tile, group * lines : group * lines + high, :
                    ]

    def convolve(part):
        for tile in range(2):

            def body(i, _, tile=tile):
                line = part * part_rows + i // (tile_cols // 8)
                col = (i % (tile_cols // 8)) * 8
                total = jnp.broadcast_to(spread(dw_bias, tile)[None], (8, GROUPS, 128))
                for up in range(KS):
                    begin = pl.multiple_of(spot_of(tile, line + up, col, 0), 8)
                    cells = pad[pl.ds(begin, GROUPS * (7 + KS)), :].reshape(7 + KS, GROUPS, 128)
                    for j in range(KS):
                        at = ((tile * KS + up) * KS + j) * GROUPS
                        total = total + cells[j : j + 8] * taps[at : at + GROUPS, :][None]
                begin = pl.multiple_of((line * tile_cols + col) * GROUPS, 64)
                conv[tile, pl.ds(begin, 8 * GROUPS), :] = total.reshape(8 * GROUPS, 128)
                return 0

            lax.fori_loop(0, group_px // 8, body, 0)

    def cells_of(part, b):
        where = pl.ds(pl.multiple_of(part * part_regs + b * BLOCK, BLOCK), BLOCK)
        return where, [conv[tile, where, :].reshape(BLOCK // 8, 8, 128) for tile in range(2)]

    def measure(part):
        def body(b, _):
            _, cells = cells_of(part, b)
            mean = jnp.sum(cells[0] + cells[1], axis=2, keepdims=True) * (1.0 / chans)
            off = [values - mean for values in cells]
            squares = jnp.sum(off[0] * off[0] + off[1] * off[1], axis=2, keepdims=True)
            lane = lax.broadcasted_iota(jnp.int32, cells[0].shape, 2)
            turned = jnp.where(lane == 0, mean, squares).reshape(BLOCK, 128).T
            stat[part, z, pl.ds(b, 1), :] = turned[0:1]
            stat[part, z, pl.ds(STATS + b, 1), :] = turned[1:2]
            return 0

        lax.fori_loop(0, STATS, body, 0)
        for step in range(1, blks):
            send(
                lambda step=step: remote(
                    stat.at[part, z], stat.at[part, z], stat_s.at[part, step], stat_r.at[part, z],
                    at_z((z + step) % blks),
                )
            )

    def columns(index):
        return pl.ds(pl.multiple_of(index * chans, chans), chans)

    def normalize(part):
        for step in range(1, blks):
            other = (z + step) % blks
            arrived(stat.at[part, other], stat_s.at[part, step], stat_r.at[part, other], at_z(other))
        mean = sum(stat[part, o, 0:STATS] for o in range(blks)) / blks
        spread_sum = sum(
            stat[part, o, STATS : 2 * STATS] + chans * (stat[part, o, 0:STATS] - mean) ** 2 for o in range(blks)
        )
        norm_stat[0] = mean
        norm_stat[1] = lax.rsqrt(spread_sum / full + 1e-06)

        def body(b, _):
            where, cells = cells_of(part, b)
            means, scales = (
                jnp.broadcast_to(norm_stat[k, pl.ds(b, 1), :], (BLOCK, 128)).T.reshape(BLOCK // 8, 8, 128)
                for k in range(2)
            )
            for tile in range(2):
                normed = (cells[tile] - means) * scales * spread(gain, tile)[None] + spread(beta, tile)[None]
                conv[tile, where, :] = normed.reshape(BLOCK, 128)
            return 0

        lax.fori_loop(0, STATS, body, 0)
        for group in range(GROUPS):
            begin = (group % per_blk) * group_px
            for tile in range(2):
                a_send[part, group // per_blk, begin : begin + group_px, tile * 128 : (tile + 1) * 128] = conv[
                    tile, pl.ds(part * part_regs + group, group_px, stride=GROUPS), :
                ].astype(jnp.bfloat16)
        pltpu.make_async_copy(
            a_send.at[part, z], act.at[part, pl.ds(0, part_px), columns(z)], a_l.at[part]
        ).start()
        send(
            lambda: remote(
                a_send.at[part, z], act.at[part, pl.ds(part_px, part_px), columns(z)],
                y_s.at[part, 0], y_r.at[part, z], mate(part),
            )
        )

    def regroup(part):
        for step in (2, 1, 3):
            send(
                lambda step=step: remote(
                    a_send.at[part, (z + step) % blks], act.at[part, pl.ds(0, part_px), columns(z)],
                    a_s.at[part, step], a_r.at[part, z], at_z((z + step) % blks),
                )
            )

    def swap_rows(part):
        for step in (1, 3, 2):
            other = (z + step) % blks
            held = act.at[part, pl.ds(0, part_px), columns(other)]
            arrived(held, a_s.at[part, step], a_r.at[part, other], at_z(other))
            send(
                lambda other=other, step=step: remote(
                    act.at[part, pl.ds(0, part_px), columns(other)],
                    act.at[part, pl.ds(part_px, part_px), columns(other)],
                    y_s.at[part, step], y_r.at[part, other], mate(part),
                )
            )
        pltpu.make_async_copy(
            a_send.at[part, z], act.at[part, pl.ds(0, part_px), columns(z)], a_l.at[part]
        ).wait()

    def both_ways(dist):
        return ((z >= dist, lambda: z - dist, z < blks - 1, 1), (z + dist < blks, lambda: z + dist, z > 0, -1))

    def passed_on(dist, k):
        for cond, origin, more, step in both_ways(dist):
            spot = lambda origin=origin: spot_for(k, origin(), 0, c)
            yield cond & more, lambda spot=spot, origin=origin, step=step: remote(
                spot(), spot(), zfwd_s.at[k, origin()], z_r.at[k, origin()], at_z(z + step)
            )

    def forward(dist, k):
        for cond, make in (pair for j in each(k) for pair in passed_on(dist, j)):
            when(cond, lambda make=make: make().start())

    def forwarded(dist, k):
        for cond, make in (pair for j in each(k) for pair in passed_on(dist, j)):
            when(cond, lambda make=make: make().wait_send())

    def take_in(dist, k):
        for j in each(k):
            take_piece(dist, j)

    def take_piece(dist, k):
        for cond, origin, _, _ in both_ways(dist):
            spot = lambda origin=origin: spot_for(k, origin(), 0, c)
            when(
                cond,
                lambda spot=spot, origin=origin: arrived(spot(), zown_s.at[k, 0], z_r.at[k, origin()], side),
            )
            for n, device in ((1, side), (2, partner)):
                send(
                    lambda spot=spot, origin=origin, n=n, device=device: remote(
                        spot(), spot_for(k, origin(), n, c), x_s.at[k, n - 1, origin()], x_r.at[k, n - 1, origin()],
                        device,
                    ),
                    cond,
                )
            send(
                lambda spot=spot, origin=origin: remote(
                    spot(), spot(), c_s.at[k, 0, origin()], c_r.at[k, 0, origin()], sibling
                ),
                cond,
            )

    def share(dist, k):
        for j in each(k):
            share_piece(dist, j)

    def share_piece(dist, k):
        for cond, origin, _, _ in both_ways(dist):
            for n, device in ((1, side), (2, partner)):
                spot = lambda origin=origin, n=n: spot_for(k, origin(), n, c)
                when(
                    cond,
                    lambda spot=spot, origin=origin, n=n, device=device: arrived(
                        spot(), x_s.at[k, n - 1, origin()], x_r.at[k, n - 1, origin()], device
                    ),
                )
                send(
                    lambda spot=spot, origin=origin, n=n: remote(
                        spot(), spot(), c_s.at[k, n, origin()], c_r.at[k, n, origin()], sibling
                    ),
                    cond,
                )

    shift = jnp.where(z < blks // 2, 0, 1)
    far = jnp.where(z < blks // 2, blks - 1, 0)

    def hold(other):
        for k in range(len(weights)):
            for n in range(3):
                arrived(spot_for(k, other, n, 1 - c), c_s.at[k, n, other], c_r.at[k, n, other], sibling)

    def early():
        for copy in own:
            copy.wait()
        for step in range(1, blks):
            other = (z + step) % blks
            arrived(b_all.at[other], bias_s.at[step], bias_r.at[other], at_z(other))
        for i in range(blks - 1):
            pl.when(i + shift != z)(lambda i=i: hold(i + shift))
        wide_rows = quarter // 128
        for o in range(blks):
            for n in range(3):
                for k in range(wide_rows):
                    bias[o, n, :, k * 128 : (k + 1) * 128] = jnp.broadcast_to(
                        b_all[o, pl.ds(quarters[n] * wide_rows + k, 1), :], (8, 128)
                    )

    def late():
        hold(far)

    def term_of(part, o):
        def hidden_of(n):
            pre_act = lax.dot_general(
                act[part], first[o, n], (((1,), (1,)), ((), ())), preferred_element_type=jnp.float32
            )
            pre_act = pre_act + bias[o, n, 0:1, :]
            return (0.5 * pre_act * (1.0 + lax.erf(pre_act * 0.7071067811865476))).astype(jnp.bfloat16)

        return sum(
            jnp.dot(hidden_of(n), second[o, n], preferred_element_type=jnp.float32) for n in (0, 1 + part % 2)
        )

    def begin_feed(part):
        for step in range(blks):
            other = (z + step) % blks
            arrived(
                act.at[part, pl.ds(part_px, part_px), columns(other)], y_s.at[part, step], y_r.at[part, other], mate(part)
            )
        for i in range(blks - 1):
            term = term_of(part, i + shift)
            acc[part] = term if i == 0 else acc[part] + term

    def end_feed(part):
        acc[part] = acc[part] + term_of(part, far)
        for n in range(per_blk):
            rows = slice(n * group_px, (n + 1) * group_px)
            p_send[part, rows, :] = acc[part, part_px + n * group_px : part_px + (n + 1) * group_px, :].astype(
                jnp.bfloat16
            )
            send(
                lambda n=n: remote(
                    p_send.at[part, pl.ds(n * group_px, group_px)], p_in.at[part, pl.ds(n * group_px, group_px)],
                    p_s.at[part, n], p_r.at[part, n], mate(part),
                )
            )

    def result_rows(owner, part, n):
        begin = owner * (per_blk * lines * tile_cols) + n * (lines * tile_cols) + part * group_px
        return out.at[pl.ds(pl.multiple_of(begin, group_px), group_px)]

    def sums_for(owner, part, n):
        return r_send.at[part, pl.ds(n * group_px, group_px), columns(owner)]

    def give_back(part):
        for n in range(per_blk):
            rows = slice(n * group_px, (n + 1) * group_px)
            arrived(p_in.at[part, pl.ds(n * group_px, group_px)], p_s.at[part, n], p_r.at[part, n], mate(part))
            r_send[part, rows, :] = (acc[part, rows, :] + p_in[part, rows, :].astype(jnp.float32)).astype(jnp.bfloat16)
            for step in range(1, blks):
                send(
                    lambda step=step, n=n: remote(
                        sums_for((z + step) % blks, part, n), result_rows(z, part, n),
                        r_s.at[part, n, step], r_r.at[part, n, z], at_z((z + step) % blks),
                    )
                )
            pltpu.make_async_copy(sums_for(z, part, n), result_rows(z, part, n), r_l.at[part, n]).start()

    def collect(part):
        for n in range(per_blk):
            for step in range(1, blks):
                other = (z + step) % blks
                arrived(result_rows(other, part, n), r_s.at[part, n, step], r_r.at[part, n, other], at_z(other))
            pltpu.make_async_copy(sums_for(z, part, n), result_rows(z, part, n), r_l.at[part, n]).wait()

    own_gone(0)
    own_out(1)
    take_in(1, 0)
    finish_halo()
    convolve(0)
    measure(0)
    own_gone(1)
    forward(1, 0)
    take_in(1, 1)
    convolve(1)
    measure(1)
    normalize(0)
    forwarded(1, 0)
    forward(1, 1)
    take_in(2, 0)
    share(1, 0)
    convolve(2)
    measure(2)
    normalize(1)
    forwarded(1, 1)
    forward(2, 0)
    take_in(2, 1)
    regroup(0)
    share(1, 1)
    convolve(3)
    measure(3)
    normalize(2)
    forwarded(2, 0)
    forward(2, 1)
    take_in(3, 0)
    share(2, 0)
    normalize(3)
    swap_rows(0)
    regroup(1)
    forwarded(2, 1)
    take_in(3, 1)
    share(2, 1)
    share(3, 0)
    swap_rows(1)
    regroup(2)
    share(3, 1)
    swap_rows(2)
    regroup(3)
    early()
    begin_feed(0)
    late()
    end_feed(0)
    begin_feed(1)
    end_feed(1)
    swap_rows(3)
    give_back(0)
    begin_feed(2)
    end_feed(2)
    give_back(1)
    begin_feed(3)
    end_feed(3)
    give_back(2)
    give_back(3)
    for part in range(PARTS):
        collect(part)
    for make, cond in sent:
        when(cond, lambda make=make: make().wait_send())


def fused(pixels, dw_kernel, dw_bias, ln_gain, ln_bias, w_in, b_in, w_out, b_out, layer_scale):
    tile_rows, tile_cols, chans = pixels.shape
    blks = lax.axis_size("blk")
    full = blks * chans
    hidden = w_in.shape[0]
    lines = tile_rows // GROUPS
    part_px = tile_rows * tile_cols // (blks * PARTS)
    pairs = GROUPS // blks
    high, wide = lines + 2 * REACH, tile_cols + 2 * REACH
    vmem, dma = pltpu.VMEM, pltpu.SemaphoreType.DMA
    anywhere = pl.BlockSpec(memory_space=pl.ANY)
    bf16, f32 = jnp.bfloat16, jnp.float32
    summed = pl.pallas_call(
        fused_kernel,
        in_specs=[pl.BlockSpec(memory_space=pltpu.HBM)] * 8,
        out_specs=anywhere,
        out_shape=jax.ShapeDtypeStruct((tile_rows * tile_cols, chans), bf16),
        scratch_shapes=[
            vmem(pixels.shape, bf16),
            vmem(dw_kernel.shape, f32),
            vmem((1, chans), f32),
            vmem((1, chans), f32),
            vmem((1, chans), f32),
            vmem((hidden // 128, 128), bf16),
            vmem((blks, hidden // 128, 128), f32),
            dma((6,)),
            vmem((2 * high * wide * GROUPS, 128), f32),
            vmem((2 * KS * KS * GROUPS, 128), f32),
            vmem((2, lines * tile_cols * GROUPS, 128), f32),
            vmem((REACH, tile_rows, chans), bf16),
            vmem((REACH, tile_rows, chans), bf16),
            vmem((2, REACH, tile_cols, chans), bf16),
            vmem((2, REACH, 16, chans), bf16),
            vmem((REACH, 2, tile_rows + 8, 128), f32),
            vmem((PARTS, blks, 2 * STATS, 128), f32),
            vmem((2, STATS, 128), f32),
            vmem((blks, 3, 8, hidden // 4), f32),
            vmem((blks, 3, hidden // 4, full), bf16),
            vmem((blks, 3, hidden // 4, full), bf16),
            vmem((PARTS, blks, part_px, chans), bf16),
            vmem((PARTS, 2 * part_px, full), bf16),
            vmem((PARTS, 2 * part_px, full), f32),
            vmem((PARTS, part_px, full), bf16),
            vmem((PARTS, part_px, full), bf16),
            vmem((PARTS, part_px, full), bf16),
            dma((2, 3)), dma((5,)), dma((5,)), dma((blks,)), dma((blks,)), dma((PARTS, blks)), dma((PARTS, blks)),
            dma((2 * CUTS, 2)), dma((2 * CUTS, blks)), dma((2 * CUTS, blks)),
            dma((2 * CUTS, 2, blks)), dma((2 * CUTS, 2, blks)), dma((2 * CUTS, 3, blks)), dma((2 * CUTS, 3, blks)),
            dma((PARTS, blks)), dma((PARTS, blks)), dma((PARTS,)),
            dma((PARTS, blks)), dma((PARTS, blks)), dma((PARTS, pairs)), dma((PARTS, pairs)),
            dma((PARTS, pairs, blks)), dma((PARTS, pairs, blks)), dma((PARTS, pairs)),
        ],
        compiler_params=pltpu.CompilerParams(
            collective_id=0, has_side_effects=True, vmem_limit_bytes=64 * 1024 * 1024
        ),
    )(
        pixels, dw_kernel, dw_bias[None, :], ln_gain[None, :], ln_bias[None, :],
        b_in.reshape(hidden // 128, 128), w_in, w_out,
    )
    result = pixels.astype(f32) + layer_scale * (
        summed.astype(f32).reshape(tile_rows, tile_cols, chans) + b_out
    )
    return result.astype(bf16)


def shards(pixels, *params):
    tile_rows, tile_cols, chans = pixels.shape
    blks = lax.axis_size("blk")
    fits = (
        (lax.axis_size("y"), lax.axis_size("col"), blks, chans) == (2, 2, 4, 256)
        and (tile_rows, tile_cols) == (64, 32)
        and params[4].shape[0] % 1024 == 0
    )
    return (fused if fits else general)(pixels, *params)


def solution(mesh):
    row, col, blk = (mesh.shape[name] for name in ("row", "col", "blk"))
    split = Mesh(mesh.devices.reshape(row // 2, 2, col, blk), ("y", "core", "col", "blk"))
    placed = (
        P(("y", "core"), "col", "blk"),
        P(None, None, "blk"),
        P("blk"),
        P("blk"),
        P("blk"),
        P("blk", None),
        P("blk"),
        P("blk", None),
        P("blk"),
        P("blk"),
    )
    return jax.shard_map(
        shards, mesh=split, in_specs=placed, out_specs=P(("y", "core"), "col", "blk"), check_vma=False
    )
```
